256 devices in a mesh: row: 64 (over z, y, core), col: 4 (over x).
Axes of the slice: x: 4, y: 4, z: 8, core: 2. Of those that a mesh axis runs over, the one named last changes fastest.
Arguments:
- source: bfloat16 [16384, 256], P('row'), may hold values from -6 to 6
- target: bfloat16 [16384, 256], P('col'), may hold values from -6 to 6
Outputs:
- row_potential: float32 [16384], P('row')
- column_potential: float32 [16384], P('col')
The draws below stay inside these ranges and needn't reach their ends.
All inputs are finite; a program needn't handle non-finite values.
Results may differ from the reference program's by a relative error of at most 0.0003.
Values sent between devices are 32-bit elements; how exact they have to be, the bound alone decides.
No kernel may reach another device: no remote copies, remote signals or barrier semaphores. Data moves between devices by JAX's collectives and lax.ppermute only.
A program may use at most 64 MiB of HBM per device.

```python
import math
import jax
import jax.numpy as jnp
from jax import lax

W = 256
ITERS = 4
ROWS = 16384
COLS = 16384


def draw_target(key, part):
    own_key = jax.random.fold_in(key, 2)
    return jnp.clip(jax.random.normal(own_key, (COLS, W), jnp.float32), -6.0, 6.0).astype(jnp.bfloat16)


def draw_source(key, part):
    own_key = jax.random.fold_in(key, 3)
    return jnp.clip(jax.random.normal(own_key, (ROWS, W), jnp.float32), -6.0, 6.0).astype(jnp.bfloat16)


def setup_inputs(seed: int = 0) -> dict:
    arg_keys = jax.random.split(jax.random.key(seed), 3)
    source = draw_source(jax.random.fold_in(arg_keys[2], 71), 0)
    target = draw_target(jax.random.fold_in(arg_keys[2], 71), 0)
    return dict(source=source, target=target)


epsilon = 0.1

def cost_block(rows, target):
    return -jnp.dot(rows, target.T, preferred_element_type=jnp.float32) * (1.0 / math.sqrt(W))

def reference(source, target):
    block = min(1024, ROWS)
    count = ROWS // block
    blocks = source.reshape(count, block, W)
    column_potential = jnp.zeros((COLS,), jnp.float32)
    row_potential = jnp.zeros((ROWS,), jnp.float32)
    for step in range(ITERS):

        def row_update(rows):
            scores = (column_potential[None, :] - cost_block(rows, target)) / epsilon
            peak = lax.optimization_barrier(jnp.max(scores, axis=1))
            total = lax.optimization_barrier(jnp.sum(jnp.exp(scores - peak[:, None]), axis=1))
            return epsilon * math.log(COLS) - epsilon * (peak + jnp.log(total))
        row_potential = lax.map(row_update, blocks).reshape(ROWS)
        pots = row_potential.reshape(count, block)

        def column_step(carry, item):
            rows, pot = item
            scores = (pot[:, None] - cost_block(rows, target)) / epsilon
            peak = jnp.maximum(carry[0], lax.optimization_barrier(jnp.max(scores, axis=0)))
            total = carry[1] * jnp.exp(carry[0] - peak) + lax.optimization_barrier(jnp.sum(jnp.exp(scores - peak[None, :]), axis=0))
            return ((peak, total), None)
        start = (jnp.full((COLS,), -jnp.inf, jnp.float32), jnp.zeros((COLS,), jnp.float32))
        (peak, total), unused = lax.scan(column_step, start, (blocks, pots))
        column_potential = epsilon * math.log(ROWS) - epsilon * (peak + jnp.log(total))
    return (row_potential, column_potential)
```

```python
import math

import jax
import jax.numpy as jnp
from jax import lax
from jax.experimental import pallas as pl
from jax.experimental.pallas import tpu as pltpu
from jax.sharding import Mesh, PartitionSpec as P

ITERS = 4
EPSILON = 0.1
TILE = 256
LANES = 128

PLANE = ("z", "y")
LINE = ("core", "x")


def combine(parts):
    peak = jnp.max(parts, axis=0, keepdims=True)
    return peak + jnp.log2(jnp.sum(jnp.exp2(parts - peak), axis=0, keepdims=True))


def row_half(scale, bits, source_ref, target_ref, *refs):
    if len(refs) == 4:
        gathered_ref, out_ref, scores, peaks = refs
        potential = bits - combine(gathered_ref[...])
    else:
        out_ref, scores, peaks = refs
        potential = None
    source = source_ref[...]
    rows, cols = source.shape[0], target_ref.shape[0]
    for start in range(0, cols, TILE):
        tile = slice(start, start + TILE)
        part = lax.dot_general(
            source, target_ref[tile, :], (((1,), (1,)), ((), ())), preferred_element_type=jnp.float32
        ) * scale
        if potential is not None:
            part = part + potential[:, tile]
        scores[:, tile] = part
        high = part[:, :LANES]
        for lane in range(LANES, TILE, LANES):
            high = jnp.maximum(high, part[:, lane : lane + LANES])
        peaks[...] = high if start == 0 else jnp.maximum(peaks[...], high)
    for start in range(0, rows, LANES):
        block = slice(start, start + LANES)
        peak = jnp.max(peaks[block, :], axis=1, keepdims=True)
        total = jnp.sum(jnp.exp2(scores[block, :] - peak), axis=1, keepdims=True)
        result = peak + jnp.log2(total)
        turned = jnp.broadcast_to(result, (LANES, LANES)).T
        out_ref[:, block] = jnp.broadcast_to(turned[:1], (out_ref.shape[0], LANES))


def column_half(scale, bits, source_ref, target_ref, gathered_ref, out_ref, row_ref):
    potential = bits - combine(gathered_ref[...])
    row_ref[...] = potential
    rows, cols = source_ref.shape[0], target_ref.shape[0]
    turned = jnp.concatenate(
        [
            jnp.broadcast_to(potential[:, start : start + LANES], (LANES, LANES)).T
            for start in range(0, rows, LANES)
        ],
        axis=0,
    )
    turned = jnp.concatenate([turned] * (TILE // LANES), axis=1)
    source = source_ref[...]
    for start in range(0, cols, TILE):
        tile = slice(start, start + TILE)
        part = lax.dot_general(
            source, target_ref[tile, :], (((1,), (1,)), ((), ())), preferred_element_type=jnp.float32
        ) * scale + turned
        peak = jnp.max(part, axis=0, keepdims=True)
        total = jnp.sum(jnp.exp2(part - peak), axis=0, keepdims=True)
        out_ref[:, tile] = jnp.broadcast_to(peak + jnp.log2(total), (out_ref.shape[0], TILE))


def widen(source_ref, out_ref):
    out_ref[...] = source_ref[...].astype(jnp.float32)


def gather(core_ref, mine_ref, other_ref, target_ref, source_out, target_out):
    core = core_ref[0]
    rows = mine_ref.shape[0]
    half = target_out.shape[0]
    mine = mine_ref[...]
    other = other_ref[...]
    source_out[:rows, :] = jnp.where(core == 0, mine, other).astype(jnp.bfloat16)
    source_out[rows:, :] = jnp.where(core == 0, other, mine).astype(jnp.bfloat16)
    target_out[...] = target_ref[pl.ds(pl.multiple_of(core * half, half), half), :]


def local(source, target):
    width = source.shape[1]
    plane = lax.axis_size(PLANE)
    line = lax.axis_size(LINE)
    rows = source.shape[0] * lax.axis_size("core")
    cols = target.shape[0] // lax.axis_size("core")
    row_bits = math.log2(rows * plane)
    col_bits = math.log2(cols * line)
    scale = math.log2(math.e) / (math.sqrt(width) * EPSILON)
    unit = EPSILON * math.log(2.0)
    limit = pltpu.CompilerParams(vmem_limit_bytes=40 * 2**20)
    core = lax.axis_index("core")
    vmem = pl.BlockSpec(memory_space=pltpu.VMEM)

    mine = pl.pallas_call(
        widen, out_shape=jax.ShapeDtypeStruct(source.shape, jnp.float32), name="widen"
    )(source)
    other = lax.ppermute(mine, "core", [(0, 1), (1, 0)])
    source, target = pl.pallas_call(
        gather,
        in_specs=[pl.BlockSpec(memory_space=pltpu.SMEM), vmem, vmem, vmem],
        out_specs=[vmem, vmem],
        out_shape=[
            jax.ShapeDtypeStruct((rows, width), jnp.bfloat16),
            jax.ShapeDtypeStruct((cols, width), jnp.bfloat16),
        ],
        name="gather",
    )(core.reshape(1), mine, other, target)

    def row_call(*gathered):
        return pl.pallas_call(
            lambda *refs: row_half(scale, row_bits, *refs),
            in_specs=[vmem] * (2 + len(gathered)),
            out_specs=vmem,
            out_shape=jax.ShapeDtypeStruct((line, rows), jnp.float32),
            scratch_shapes=[
                pltpu.VMEM((rows, cols), jnp.float32),
                pltpu.VMEM((rows, LANES), jnp.float32),
            ],
            compiler_params=limit,
            name="row_half",
        )(source, target, *gathered)

    def column_call(gathered):
        return pl.pallas_call(
            lambda *refs: column_half(scale, col_bits, *refs),
            in_specs=[vmem] * 3,
            out_specs=[vmem, vmem],
            out_shape=[
                jax.ShapeDtypeStruct((plane, cols), jnp.float32),
                jax.ShapeDtypeStruct((1, rows), jnp.float32),
            ],
            compiler_params=limit,
            name="column_half",
        )(source, target, gathered)

    columns = None
    for step in range(ITERS):
        parts = row_call() if columns is None else row_call(columns)
        gathered = lax.all_to_all(parts, LINE, 0, 0)
        parts, row_potential = column_call(gathered)
        columns = lax.all_to_all(parts, PLANE, 0, 0)
    column_potential = unit * (row_bits - combine(columns)[0])
    other = lax.ppermute(column_potential, "core", [(0, 1), (1, 0)])
    column_potential = jnp.where(
        core == 0,
        jnp.concatenate([column_potential, other]),
        jnp.concatenate([other, column_potential]),
    )
    own = rows // lax.axis_size("core")
    row_potential = lax.dynamic_slice(row_potential[0], (core * own,), (own,)) * unit
    return (row_potential, column_potential)


def solution(mesh):
    fine = Mesh(mesh.devices.reshape(8, 4, 2, 4), ("z", "y", "core", "x"))
    return jax.shard_map(
        local,
        mesh=fine,
        in_specs=(P(("z", "y", "core"), None), P("x", None)),
        out_specs=(P(("z", "y", "core")), P("x")),
        check_vma=False,
    )
```

```python
import math

import jax
import jax.numpy as jnp
from jax import lax
from jax.experimental import pallas as pl
from jax.experimental.pallas import tpu as pltpu
from jax.sharding import Mesh, PartitionSpec as P

ITERS = 4
EPSILON = 0.1
TILE = 256
LANES = 128
SUBLANES = 8
CHUNKS = 4
SAFE = 2.0**-80

PLANE = ("z", "y")
LINE = ("core", "x")


def combine(parts):
    peak = jnp.max(parts, axis=0)
    return peak + jnp.log2(jnp.sum(jnp.exp2(parts - peak[None]), axis=0))


def largest(values):
    return jnp.max(jnp.max(values, axis=1, keepdims=True), axis=0, keepdims=True)


def smallest(values):
    return jnp.min(jnp.min(values, axis=1, keepdims=True), axis=0, keepdims=True)


def stand(values):
    return jnp.concatenate(
        [jnp.broadcast_to(values[k : k + 1], (LANES, LANES)).T for k in range(values.shape[0])], axis=0
    )


def spread(row, count):
    return jnp.concatenate([row] * count, axis=1)


def send(out_ref, values):
    for slot in range(out_ref.shape[0]):
        out_ref[slot] = values


def score(source, target, scale):
    return scale * lax.dot_general(
        source, target, (((1,), (1,)), ((), ())), preferred_element_type=jnp.float32
    )


def first_rows(scale, source_ref, target_ref, out_ref, wide_ref, target, scores, peaks, line, arrived):
    source = source_ref[...]
    rows, cols = source.shape[0], target.shape[0]
    chunk = cols // CHUNKS
    copies = []
    for k in range(CHUNKS):
        part = pl.ds(k * chunk, chunk)
        copies.append(pltpu.make_async_copy(target_ref.at[part], target.at[part], arrived.at[k]))
        copies[-1].start()
    wide_ref[...] = source.astype(jnp.float32)
    for start in range(0, cols, TILE):
        if start % chunk == 0:
            copies[start // chunk].wait()
        tile = slice(start, start + TILE)
        part = score(source, target[tile, :], scale)
        scores[:, tile] = part
        high = part[:, :LANES]
        for lane in range(LANES, TILE, LANES):
            high = jnp.maximum(high, part[:, lane : lane + LANES])
        peaks[...] = high if start == 0 else jnp.maximum(peaks[...], high)
    for k in range(rows // LANES):
        block = slice(k * LANES, (k + 1) * LANES)
        peak = jnp.max(peaks[block, :], axis=1, keepdims=True)
        total = jnp.sum(jnp.exp2(scores[block, :] - peak), axis=1, keepdims=True)
        line[k : k + 1, :] = jnp.broadcast_to(peak + jnp.log2(total), (LANES, LANES)).T[:1]
    send(out_ref, line[...])


def all_scores(scale, core_ref, mine_ref, other_ref, target_ref, scores_ref, source, target, arrived):
    core = core_ref[0]
    rows = mine_ref.shape[0]
    cols = target.shape[0]
    chunk = cols // CHUNKS
    copies = []
    for k in range(CHUNKS):
        copies.append(
            pltpu.make_async_copy(
                target_ref.at[pl.ds(pl.multiple_of(core * cols + k * chunk, chunk), chunk)],
                target.at[pl.ds(k * chunk, chunk)],
                arrived.at[k],
            )
        )
        copies[-1].start()
    mine = mine_ref[...].astype(jnp.float32)
    other = other_ref[...]
    source[:rows, :] = jnp.where(core == 0, mine, other).astype(jnp.bfloat16)
    source[rows:, :] = jnp.where(core == 0, other, mine).astype(jnp.bfloat16)
    for start in range(0, cols, TILE):
        if start % chunk == 0:
            copies[start // chunk].wait()
        tile = slice(start, start + TILE)
        scores_ref[:, tile] = score(source[...], target[tile, :], scale)


def column_sums(rows, width, get):
    total = lax.fori_loop(
        0,
        rows // SUBLANES,
        lambda k, total: total + get(pl.ds(pl.multiple_of(k * SUBLANES, SUBLANES), SUBLANES)),
        jnp.zeros((SUBLANES, width), jnp.float32),
        unroll=8,
    )
    return jnp.sum(total, axis=0, keepdims=True)


def fold(ref, row):
    for k in range(ref.shape[0]):
        ref[k : k + 1, :] = row[:, k * LANES : (k + 1) * LANES]
    return ref[...]


def exact_columns(get, rows, width, keep=None):
    high = lax.fori_loop(
        0,
        rows // SUBLANES,
        lambda k, high: jnp.maximum(high, get(pl.ds(pl.multiple_of(k * SUBLANES, SUBLANES), SUBLANES))),
        jnp.full((SUBLANES, width), -jnp.inf, jnp.float32),
        unroll=8,
    )
    peak = jnp.max(high, axis=0, keepdims=True)
    shift = jnp.broadcast_to(peak, (SUBLANES, width))

    def term(block):
        value = jnp.exp2(get(block) - shift)
        if keep is not None:
            keep[block, :] = value
        return value

    return peak, column_sums(rows, width, term)


def first_columns(bits, scores_ref, gathered_ref, out_ref, plan_ref, row_ref, peak_ref, standing, folded):
    rows, cols = scores_ref.shape
    cores = 2
    each = gathered_ref.shape[0] // cores
    parts = gathered_ref[...]
    potential = bits - jnp.concatenate([combine(parts[k * each : (k + 1) * each]) for k in range(cores)], axis=0)
    row_ref[...] = potential
    standing[...] = stand(potential)
    peak, total = exact_columns(
        lambda block: scores_ref[block, :] + spread(standing[block, :], cols // LANES), rows, cols, plan_ref
    )
    peak = fold(peak_ref, peak)
    send(out_ref, peak + jnp.log2(fold(folded, total)))


def later_rows(
    bits, gathered_ref, plan_ref, row_ref, peak_ref, scores_ref, out_ref, factor, totals, block_scores, arrived
):
    rows, cols = plan_ref.shape
    potential = bits - combine(gathered_ref[...])
    change = potential + peak_ref[...]
    shift = largest(change)
    factor[...] = jnp.exp2(change - shift)
    for k in range(rows // LANES):
        block = slice(k * LANES, (k + 1) * LANES)
        total = jnp.zeros((LANES, LANES), jnp.float32)
        for t in range(cols // LANES):
            total = total + plan_ref[block, t * LANES : (t + 1) * LANES] * factor[t : t + 1, :]
        totals[k : k + 1, :] = jnp.sum(total.T, axis=0, keepdims=True)
    total = totals[...]
    send(out_ref, shift - row_ref[...] + jnp.log2(total))

    @pl.when(jnp.logical_not(smallest(total)[0, 0] >= SAFE))
    def _():
        factor[...] = potential
        for k in range(rows // LANES):
            block = slice(k * LANES, (k + 1) * LANES)
            copy = pltpu.make_async_copy(scores_ref.at[pl.ds(k * LANES, LANES)], block_scores, arrived)
            copy.start()
            copy.wait()
            for t in range(cols // LANES):
                tile = slice(t * LANES, (t + 1) * LANES)
                block_scores[:, tile] = block_scores[:, tile] + factor[t : t + 1, :]
            peak = jnp.max(block_scores[...], axis=1, keepdims=True)
            total = jnp.sum(jnp.exp2(block_scores[...] - peak), axis=1, keepdims=True)
            totals[k : k + 1, :] = jnp.broadcast_to(peak + jnp.log2(total), (LANES, LANES)).T[:1]
        send(out_ref, totals[...])


def later_columns(
    bits,
    gathered_ref,
    plan_ref,
    row_ref,
    peak_ref,
    scores_ref,
    out_ref,
    potential_ref,
    standing,
    folded,
    all_scores_here,
    arrived,
):
    rows, cols = plan_ref.shape
    count = cols // LANES
    potential = bits - combine(gathered_ref[...])
    potential_ref[...] = potential
    change = potential - row_ref[...]
    shift = largest(change)
    standing[...] = stand(jnp.exp2(change - shift))
    total = fold(
        folded,
        column_sums(rows, cols, lambda block: plan_ref[block, :] * spread(standing[block, :], count)),
    )
    send(out_ref, peak_ref[...] + shift + jnp.log2(total))

    @pl.when(jnp.logical_not(smallest(total)[0, 0] >= SAFE))
    def _():
        copy = pltpu.make_async_copy(scores_ref, all_scores_here, arrived)
        copy.start()
        copy.wait()
        standing[...] = stand(potential_ref[...])
        peak, total = exact_columns(
            lambda block: all_scores_here[block, :] + spread(standing[block, :], count), rows, cols
        )
        peak = fold(folded, peak)
        send(out_ref, peak + jnp.log2(fold(folded, total)))


def local(source, target):
    f32 = jnp.float32
    own, width = source.shape
    plane = lax.axis_size(PLANE)
    line = lax.axis_size(LINE)
    cores = lax.axis_size("core")
    rows = own * cores
    cols = target.shape[0] // cores
    row_bits = math.log2(rows * plane)
    col_bits = math.log2(cols * line)
    scale = math.log2(math.e) / (math.sqrt(width) * EPSILON)
    unit = EPSILON * math.log(2.0)
    core = lax.axis_index("core")
    vmem = pl.BlockSpec(memory_space=pltpu.VMEM)
    smem = pl.BlockSpec(memory_space=pltpu.SMEM)
    anywhere = pl.BlockSpec(memory_space=pl.ANY)
    row_shape = (rows // LANES, LANES)
    col_shape = (cols // LANES, LANES)
    limit = pltpu.CompilerParams(vmem_limit_bytes=32 * 2**20)

    parts, mine = pl.pallas_call(
        lambda *refs: first_rows(scale, *refs),
        in_specs=[vmem, anywhere],
        out_specs=[vmem, vmem],
        out_shape=[
            jax.ShapeDtypeStruct((line, own // LANES, LANES), f32),
            jax.ShapeDtypeStruct((own, width), f32),
        ],
        scratch_shapes=[
            pltpu.VMEM(target.shape, target.dtype),
            pltpu.VMEM((own, target.shape[0]), f32),
            pltpu.VMEM((own, LANES), f32),
            pltpu.VMEM((own // LANES, LANES), f32),
            pltpu.SemaphoreType.DMA((CHUNKS,)),
        ],
        compiler_params=limit,
        name="first_rows",
    )(source, target)
    other = lax.ppermute(mine, "core", [(0, 1), (1, 0)])
    gathered = lax.all_to_all(parts, LINE, 0, 0)
    scores = pl.pallas_call(
        lambda *refs: all_scores(scale, *refs),
        in_specs=[smem, vmem, vmem, anywhere],
        out_specs=vmem,
        out_shape=jax.ShapeDtypeStruct((rows, cols), f32),
        scratch_shapes=[
            pltpu.VMEM((rows, width), source.dtype),
            pltpu.VMEM((cols, width), target.dtype),
            pltpu.SemaphoreType.DMA((CHUNKS,)),
        ],
        compiler_params=limit,
        name="all_scores",
    )(core.reshape(1), source, other, target)
    parts, plan, row_base, peaks = pl.pallas_call(
        lambda *refs: first_columns(col_bits, *refs),
        in_specs=[vmem, vmem],
        out_specs=[vmem] * 4,
        out_shape=[
            jax.ShapeDtypeStruct((plane,) + col_shape, f32),
            jax.ShapeDtypeStruct((rows, cols), f32),
            jax.ShapeDtypeStruct(row_shape, f32),
            jax.ShapeDtypeStruct(col_shape, f32),
        ],
        scratch_shapes=[pltpu.VMEM((rows, LANES), f32), pltpu.VMEM(col_shape, f32)],
        compiler_params=limit,
        name="first_columns",
    )(scores, gathered)
    columns = lax.all_to_all(parts, PLANE, 0, 0)

    for step in range(1, ITERS):
        parts = pl.pallas_call(
            lambda *refs: later_rows(row_bits, *refs),
            in_specs=[vmem] * 4 + [anywhere],
            out_specs=vmem,
            out_shape=jax.ShapeDtypeStruct((line,) + row_shape, f32),
            scratch_shapes=[
                pltpu.VMEM(col_shape, f32),
                pltpu.VMEM(row_shape, f32),
                pltpu.VMEM((LANES, cols), f32),
                pltpu.SemaphoreType.DMA,
            ],
            compiler_params=limit,
            name="later_rows",
        )(columns, plan, row_base, peaks, scores)
        gathered = lax.all_to_all(parts, LINE, 0, 0)
        parts, row_potential = pl.pallas_call(
            lambda *refs: later_columns(col_bits, *refs),
            in_specs=[vmem] * 4 + [anywhere],
            out_specs=[vmem] * 2,
            out_shape=[
                jax.ShapeDtypeStruct((plane,) + col_shape, f32),
                jax.ShapeDtypeStruct(row_shape, f32),
            ],
            scratch_shapes=[
                pltpu.VMEM((rows, LANES), f32),
                pltpu.VMEM(col_shape, f32),
                pltpu.VMEM((rows, cols), f32),
                pltpu.SemaphoreType.DMA,
            ],
            compiler_params=limit,
            name="later_columns",
        )(gathered, plan, row_base, peaks, scores)
        columns = lax.all_to_all(parts, PLANE, 0, 0)

    column_potential = (unit * (row_bits - combine(columns))).reshape(cols)
    other = lax.ppermute(column_potential, "core", [(0, 1), (1, 0)])
    column_potential = jnp.where(
        core == 0,
        jnp.concatenate([column_potential, other]),
        jnp.concatenate([other, column_potential]),
    )
    row_potential = lax.dynamic_slice(row_potential.reshape(rows), (core * own,), (own,)) * unit
    return (row_potential, column_potential)


def solution(mesh):
    fine = Mesh(mesh.devices.reshape(8, 4, 2, 4), ("z", "y", "core", "x"))
    return jax.shard_map(
        local,
        mesh=fine,
        in_specs=(P(("z", "y", "core"), None), P("x", None)),
        out_specs=(P(("z", "y", "core")), P("x")),
        check_vma=False,
    )
```

```python
import math

import jax
import jax.numpy as jnp
from jax import lax
from jax.experimental import pallas as pl
from jax.experimental.pallas import tpu as pltpu
from jax.sharding import Mesh, PartitionSpec as P

ITERS = 4
EPSILON = 0.1
TILE = 256
LANES = 128
SUBLANES = 8
CHUNKS = 2
SAFE = 2.0**-80

PLANE = ("z", "p", "q")
ALIKE = ()
LINE = ("core", "x")


def combine(parts):
    peak = jnp.max(parts, axis=0)
    return peak + jnp.log2(jnp.sum(jnp.exp2(parts - peak[None]), axis=0))


def largest(values):
    return jnp.max(jnp.max(values, axis=1, keepdims=True), axis=0, keepdims=True)


def smallest(values):
    return jnp.min(jnp.min(values, axis=1, keepdims=True), axis=0, keepdims=True)


def stand(ref, values):
    for k in range(values.shape[0]):
        ref[k * LANES : (k + 1) * LANES, :] = jnp.broadcast_to(values[k : k + 1], (LANES, LANES)).T


def fold(ref, row):
    for k in range(ref.shape[0]):
        ref[k : k + 1, :] = row[:, k * LANES : (k + 1) * LANES]
    return ref[...]


def spread(row, count):
    return jnp.concatenate([row] * count, axis=1)


def send(out_ref, values):
    for slot in range(out_ref.shape[0]):
        out_ref[slot] = values


def score(source, target, scale):
    return scale * lax.dot_general(
        source, target, (((1,), (1,)), ((), ())), preferred_element_type=jnp.float32
    )


def first_rows(
    scale, source_ref, target_ref, out_ref, wide_ref, half_ref, source, rest, scores, peaks, line, arrived
):
    core = lax.axis_index("core")
    rows, half = source.shape[0], half_ref.shape[0]
    chunk = half // CHUNKS
    fetch = pltpu.make_async_copy(source_ref, source, arrived.at[2 * CHUNKS])
    fetch.start()
    copies = []
    for side, place in ((core, half_ref), (1 - core, rest)):
        for k in range(CHUNKS):
            copies.append(
                pltpu.make_async_copy(
                    target_ref.at[pl.ds(pl.multiple_of(side * half + k * chunk, chunk), chunk)],
                    place.at[pl.ds(k * chunk, chunk)],
                    arrived.at[len(copies)],
                )
            )
            copies[-1].start()
    fetch.wait()
    wide_ref[...] = source[...].astype(jnp.float32)
    for start in range(0, 2 * half, TILE):
        if start % chunk == 0:
            copies[start // chunk].wait()
        place = half_ref if start < half else rest
        tile = slice(start, start + TILE)
        part = score(source[...], place[start % half : start % half + TILE, :], scale)
        scores[:, tile] = part
        high = part[:, :LANES]
        for lane in range(LANES, TILE, LANES):
            high = jnp.maximum(high, part[:, lane : lane + LANES])
        peaks[...] = high if start == 0 else jnp.maximum(peaks[...], high)
    for k in range(rows // LANES):
        block = slice(k * LANES, (k + 1) * LANES)
        peak = jnp.max(peaks[block, :], axis=1, keepdims=True)
        total = jnp.sum(jnp.exp2(scores[block, :] - peak), axis=1, keepdims=True)
        line[k : k + 1, :] = jnp.broadcast_to(peak + jnp.log2(total), (LANES, LANES)).T[:1]
    send(out_ref, line[...])


def column_sums(rows, width, get):
    total = lax.fori_loop(
        0,
        rows // SUBLANES,
        lambda k, total: total + get(pl.ds(pl.multiple_of(k * SUBLANES, SUBLANES), SUBLANES)),
        jnp.zeros((SUBLANES, width), jnp.float32),
        unroll=16,
    )
    return jnp.sum(total, axis=0, keepdims=True)


def first_columns(
    scale, bits, each, *refs
):
    pieces = refs[: 2 * (1 + len(ALIKE))]
    half_ref, gathered_ref, out_ref, plan_ref, row_ref, peak_ref, source_ref, standing, folded = refs[len(pieces) :]
    rows, cols = plan_ref.shape
    own = pieces[0].shape[0]
    core = lax.axis_index("core")
    group = lax.axis_index(ALIKE) if ALIKE else 0
    for index, piece in enumerate(pieces):
        here = (core + index % 2) % 2
        there = (group + index // 2) % 2 if ALIKE else 0
        start = pl.multiple_of((there * 2 + here) * own, own)
        source_ref[pl.ds(start, own), :] = piece[...].astype(source_ref.dtype)
    parts = gathered_ref[...]
    potential = bits - jnp.concatenate(
        [combine(parts[k : k + each]) for k in range(0, parts.shape[0], each)], axis=0
    )
    row_ref[...] = potential
    stand(standing, potential)
    highs = []
    for start in range(0, cols, TILE):
        tile = slice(start, start + TILE)
        part = score(source_ref[...], half_ref[tile, :], scale) + spread(standing[...], TILE // LANES)
        plan_ref[:, tile] = part
        highs.append(jnp.max(part, axis=0, keepdims=True))
    peak = jnp.concatenate(highs, axis=1)
    shift = jnp.broadcast_to(peak, (SUBLANES, cols))

    def term(block):
        value = jnp.exp2(plan_ref[block, :] - shift)
        plan_ref[block, :] = value
        return value

    total = column_sums(rows, cols, term)
    send(out_ref, fold(peak_ref, peak) + jnp.log2(fold(folded, total)))


def later_rows(
    scale, bits, gathered_ref, plan_ref, row_ref, peak_ref, source_ref, half_ref, out_ref, factor, totals
):
    rows, cols = plan_ref.shape
    potential = bits - combine(gathered_ref[...])
    change = potential + peak_ref[...]
    shift = largest(change)
    factor[...] = jnp.exp2(change - shift)
    for k in range(rows // LANES):
        block = slice(k * LANES, (k + 1) * LANES)
        total = jnp.zeros((LANES, LANES), jnp.float32)
        for t in range(cols // LANES):
            total = total + plan_ref[block, t * LANES : (t + 1) * LANES] * factor[t : t + 1, :]
        totals[k : k + 1, :] = jnp.sum(total.T, axis=0, keepdims=True)
    total = totals[...]
    send(out_ref, shift - row_ref[...] + jnp.log2(total))

    @pl.when(jnp.logical_not(smallest(total)[0, 0] >= SAFE))
    def _():
        wide = jnp.concatenate([potential[t : t + 1] for t in range(cols // LANES)], axis=1)
        for k in range(rows // LANES):
            block = slice(k * LANES, (k + 1) * LANES)
            part = score(source_ref[block, :], half_ref[...], scale) + wide
            peak = jnp.max(part, axis=1, keepdims=True)
            total = jnp.sum(jnp.exp2(part - peak), axis=1, keepdims=True)
            totals[k : k + 1, :] = jnp.broadcast_to(peak + jnp.log2(total), (LANES, LANES)).T[:1]
        send(out_ref, totals[...])


def later_columns(
    scale, bits, gathered_ref, plan_ref, row_ref, peak_ref, source_ref, half_ref, out_ref, potential_ref, standing, folded
):
    rows, cols = plan_ref.shape
    potential = bits - combine(gathered_ref[...])
    potential_ref[...] = potential
    change = potential - row_ref[...]
    shift = largest(change)
    stand(standing, jnp.exp2(change - shift))
    total = fold(
        folded,
        column_sums(rows, cols, lambda block: plan_ref[block, :] * spread(standing[block, :], cols // LANES)),
    )
    send(out_ref, peak_ref[...] + shift + jnp.log2(total))

    @pl.when(jnp.logical_not(smallest(total)[0, 0] >= SAFE))
    def _():
        stand(standing, potential_ref[...])
        for start in range(0, cols, TILE):
            part = score(source_ref[...], half_ref[start : start + TILE, :], scale) + spread(
                standing[...], TILE // LANES
            )
            peak = jnp.max(part, axis=0, keepdims=True)
            result = peak + jnp.log2(jnp.sum(jnp.exp2(part - peak), axis=0, keepdims=True))
            for lane in range(0, TILE, LANES):
                t = (start + lane) // LANES
                folded[t : t + 1, :] = result[:, lane : lane + LANES]
        send(out_ref, folded[...])


def local(source, target):
    f32 = jnp.float32
    own, width = source.shape
    plane = lax.axis_size(PLANE)
    line = lax.axis_size(LINE)
    cores = lax.axis_size("core")
    alike = lax.axis_size(ALIKE) if ALIKE else 1
    rows = own * cores * alike
    cols = target.shape[0] // cores
    row_bits = math.log2(rows * plane)
    col_bits = math.log2(cols * line)
    scale = math.log2(math.e) / (math.sqrt(width) * EPSILON)
    unit = EPSILON * math.log(2.0)
    core = lax.axis_index("core")
    swap = [(0, 1), (1, 0)]
    vmem = pl.BlockSpec(memory_space=pltpu.VMEM)
    hbm = pl.BlockSpec(memory_space=pltpu.HBM)
    row_shape = (rows // LANES, LANES)
    col_shape = (cols // LANES, LANES)
    limit = pltpu.CompilerParams(vmem_limit_bytes=32 * 2**20)

    parts, mine, half = pl.pallas_call(
        lambda *refs: first_rows(scale, *refs),
        in_specs=[hbm, hbm],
        out_specs=[vmem, vmem, vmem],
        out_shape=[
            jax.ShapeDtypeStruct((alike * line, own // LANES, LANES), f32),
            jax.ShapeDtypeStruct((own, width), f32),
            jax.ShapeDtypeStruct((cols, width), target.dtype),
        ],
        scratch_shapes=[
            pltpu.VMEM(source.shape, source.dtype),
            pltpu.VMEM((cols, width), target.dtype),
            pltpu.VMEM((own, target.shape[0]), f32),
            pltpu.VMEM((own, LANES), f32),
            pltpu.VMEM((own // LANES, LANES), f32),
            pltpu.SemaphoreType.DMA((2 * CHUNKS + 1,)),
        ],
        compiler_params=limit,
        name="first_rows",
    )(source, target)
    pieces = [mine]
    if ALIKE:
        pieces.append(lax.ppermute(mine, ALIKE, swap))
    pieces = [form for piece in pieces for form in (piece, lax.ppermute(piece, "core", swap))]
    gathered = lax.all_to_all(parts, ALIKE + LINE, 0, 0)
    parts, plan, row_base, peaks, source = pl.pallas_call(
        lambda *refs: first_columns(scale, col_bits, line // cores, *refs),
        in_specs=[vmem] * (len(pieces) + 2),
        out_specs=[vmem] * 5,
        out_shape=[
            jax.ShapeDtypeStruct((plane,) + col_shape, f32),
            jax.ShapeDtypeStruct((rows, cols), f32),
            jax.ShapeDtypeStruct(row_shape, f32),
            jax.ShapeDtypeStruct(col_shape, f32),
            jax.ShapeDtypeStruct((rows, width), source.dtype),
        ],
        scratch_shapes=[pltpu.VMEM((rows, LANES), f32), pltpu.VMEM(col_shape, f32)],
        compiler_params=limit,
        name="first_columns",
    )(*pieces, half, gathered)
    columns = lax.all_to_all(parts, PLANE, 0, 0)

    for step in range(1, ITERS):
        parts = pl.pallas_call(
            lambda *refs: later_rows(scale, row_bits, *refs),
            in_specs=[vmem] * 6,
            out_specs=vmem,
            out_shape=jax.ShapeDtypeStruct((line,) + row_shape, f32),
            scratch_shapes=[pltpu.VMEM(col_shape, f32), pltpu.VMEM(row_shape, f32)],
            compiler_params=limit,
            name="later_rows",
        )(columns, plan, row_base, peaks, source, half)
        gathered = lax.all_to_all(parts, LINE, 0, 0)
        last = step == ITERS - 1
        outs = [jax.ShapeDtypeStruct((plane,) + col_shape, f32)]
        scratch = [pltpu.VMEM((rows, LANES), f32), pltpu.VMEM(col_shape, f32)]
        if last:
            outs.append(jax.ShapeDtypeStruct(row_shape, f32))
        else:
            scratch.insert(0, pltpu.VMEM(row_shape, f32))
        parts, *row_potential = pl.pallas_call(
            lambda *refs: later_columns(scale, col_bits, *refs),
            in_specs=[vmem] * 6,
            out_specs=[vmem] * len(outs),
            out_shape=outs,
            scratch_shapes=scratch,
            compiler_params=limit,
            name="later_columns",
        )(gathered, plan, row_base, peaks, source, half)
        columns = lax.all_to_all(parts, PLANE, 0, 0)

    column_potential = (unit * (row_bits - combine(columns))).reshape(cols)
    other = lax.ppermute(column_potential, "core", swap)
    column_potential = jnp.where(
        core == 0,
        jnp.concatenate([column_potential, other]),
        jnp.concatenate([other, column_potential]),
    )
    start = lax.axis_index(ALIKE + ("core",)) * own
    row_potential = lax.dynamic_slice(row_potential[0].reshape(rows), (start,), (own,)) * unit
    return (row_potential, column_potential)


def solution(mesh):
    fine = Mesh(mesh.devices.reshape(8, 2, 2, 2, 4), ("z", "p", "q", "core", "x"))
    return jax.shard_map(
        local,
        mesh=fine,
        in_specs=(P(("z", "p", "q", "core"), None), P("x", None)),
        out_specs=(P(("z", "p", "q", "core")), P("x")),
        check_vma=False,
    )
```

```python
import math

import jax
import jax.numpy as jnp
from jax import lax
from jax.experimental import pallas as pl
from jax.experimental.pallas import tpu as pltpu
from jax.sharding import Mesh, PartitionSpec as P

ITERS = 4
EPSILON = 0.1
TILE = 256
LANES = 128
SUBLANES = 8
CHUNKS = 2
SAFE = 2.0**-80

PLANE = ("z", "p", "q")
ALIKE = ()
LINE = ("core", "x")


def combine(parts):
    peak = jnp.max(parts, axis=0)
    return peak + jnp.log2(jnp.sum(jnp.exp2(parts - peak[None]), axis=0))


def largest(values):
    return jnp.max(jnp.max(values, axis=1, keepdims=True), axis=0, keepdims=True)


def smallest(values):
    return jnp.min(jnp.min(values, axis=1, keepdims=True), axis=0, keepdims=True)


def stand(ref, values):
    for k in range(values.shape[0]):
        ref[k * LANES : (k + 1) * LANES, :] = jnp.broadcast_to(values[k : k + 1], (LANES, LANES)).T


def fold(ref, row):
    for k in range(ref.shape[0]):
        ref[k : k + 1, :] = row[:, k * LANES : (k + 1) * LANES]
    return ref[...]


def spread(row, count):
    return jnp.concatenate([row] * count, axis=1)


def send(out_ref, values):
    for slot in range(out_ref.shape[0]):
        out_ref[slot] = values


def score(source, target, scale):
    return scale * lax.dot_general(
        source, target, (((1,), (1,)), ((), ())), preferred_element_type=jnp.float32
    )


def first_rows(
    scale, source_ref, target_ref, out_ref, wide_ref, half_ref, source, rest, scores, peaks, line, arrived
):
    core = lax.axis_index("core")
    rows, half = source.shape[0], half_ref.shape[0]
    chunk = half // CHUNKS
    fetch = pltpu.make_async_copy(source_ref, source, arrived.at[2 * CHUNKS])
    fetch.start()
    copies = []
    for side, place in ((core, half_ref), (1 - core, rest)):
        for k in range(CHUNKS):
            copies.append(
                pltpu.make_async_copy(
                    target_ref.at[pl.ds(pl.multiple_of(side * half + k * chunk, chunk), chunk)],
                    place.at[pl.ds(k * chunk, chunk)],
                    arrived.at[len(copies)],
                )
            )
            copies[-1].start()
    fetch.wait()
    wide_ref[...] = source[...].astype(jnp.float32)
    for start in range(0, 2 * half, TILE):
        if start % chunk == 0:
            copies[start // chunk].wait()
        place = half_ref if start < half else rest
        tile = slice(start, start + TILE)
        part = score(source[...], place[start % half : start % half + TILE, :], scale)
        scores[:, tile] = part
        high = part[:, :LANES]
        for lane in range(LANES, TILE, LANES):
            high = jnp.maximum(high, part[:, lane : lane + LANES])
        peaks[...] = high if start == 0 else jnp.maximum(peaks[...], high)
    for k in range(rows // LANES):
        block = slice(k * LANES, (k + 1) * LANES)
        peak = jnp.max(peaks[block, :], axis=1, keepdims=True)
        total = jnp.sum(jnp.exp2(scores[block, :] - peak), axis=1, keepdims=True)
        line[k : k + 1, :] = jnp.broadcast_to(peak + jnp.log2(total), (LANES, LANES)).T[:1]
    send(out_ref, line[...])


def column_sums(rows, width, get):
    total = lax.fori_loop(
        0,
        rows // SUBLANES,
        lambda k, total: total + get(pl.ds(pl.multiple_of(k * SUBLANES, SUBLANES), SUBLANES)),
        jnp.zeros((SUBLANES, width), jnp.float32),
        unroll=16,
    )
    return jnp.sum(total, axis=0, keepdims=True)


def first_columns(scale, bits, each, *refs):
    pieces = refs[: 2 * (1 + len(ALIKE))]
    half_ref, gathered_ref, out_ref, plan_ref, row_ref, peak_ref, source_ref, standing, folded = refs[len(pieces) :]
    rows, cols = plan_ref.shape
    own = pieces[0].shape[0]
    core = lax.axis_index("core")
    group = lax.axis_index(ALIKE) if ALIKE else 0
    for index, piece in enumerate(pieces):
        here = (core + index % 2) % 2
        there = (group + index // 2) % 2 if ALIKE else 0
        start = pl.multiple_of((there * 2 + here) * own, own)
        source_ref[pl.ds(start, own), :] = piece[...].astype(source_ref.dtype)
    parts = gathered_ref[...]
    potential = bits - jnp.concatenate(
        [combine(parts[k : k + each]) for k in range(0, parts.shape[0], each)], axis=0
    )
    row_ref[...] = potential
    stand(standing, potential)
    highs = []
    for start in range(0, cols, TILE):
        tile = slice(start, start + TILE)
        part = score(source_ref[...], half_ref[tile, :], scale) + spread(standing[...], TILE // LANES)
        plan_ref[:, tile] = part
        highs.append(jnp.max(part, axis=0, keepdims=True))
    peak = jnp.concatenate(highs, axis=1)
    shift = jnp.broadcast_to(peak, (SUBLANES, cols))

    def term(block):
        value = jnp.exp2(plan_ref[block, :] - shift)
        plan_ref[block, :] = value
        return value

    total = column_sums(rows, cols, term)
    send(out_ref, fold(peak_ref, peak) + jnp.log2(fold(folded, total)))


def later_rows(
    scale, bits, gathered_ref, plan_ref, row_ref, peak_ref, source_ref, half_ref, out_ref, factor, totals
):
    rows, cols = plan_ref.shape
    potential = bits - combine(gathered_ref[...])
    change = potential + peak_ref[...]
    shift = largest(change)
    factor[...] = jnp.exp2(change - shift)
    for k in range(rows // LANES):
        block = slice(k * LANES, (k + 1) * LANES)
        total = jnp.zeros((LANES, LANES), jnp.float32)
        for t in range(cols // LANES):
            total = total + plan_ref[block, t * LANES : (t + 1) * LANES] * factor[t : t + 1, :]
        totals[k : k + 1, :] = jnp.sum(total.T, axis=0, keepdims=True)
    total = totals[...]
    send(out_ref, shift - row_ref[...] + jnp.log2(total))

    @pl.when(jnp.logical_not(smallest(total)[0, 0] >= SAFE))
    def _():
        wide = jnp.concatenate([potential[t : t + 1] for t in range(cols // LANES)], axis=1)
        for k in range(rows // LANES):
            block = slice(k * LANES, (k + 1) * LANES)
            part = score(source_ref[block, :], half_ref[...], scale) + wide
            peak = jnp.max(part, axis=1, keepdims=True)
            total = jnp.sum(jnp.exp2(part - peak), axis=1, keepdims=True)
            totals[k : k + 1, :] = jnp.broadcast_to(peak + jnp.log2(total), (LANES, LANES)).T[:1]
        send(out_ref, totals[...])


def later_columns(
    scale, bits, gathered_ref, plan_ref, row_ref, peak_ref, source_ref, half_ref, out_ref, standing, folded
):
    rows, cols = plan_ref.shape
    potential = bits - combine(gathered_ref[...])
    change = potential - row_ref[...]
    shift = largest(change)
    stand(standing, jnp.exp2(change - shift))
    total = fold(
        folded,
        column_sums(rows, cols, lambda block: plan_ref[block, :] * spread(standing[block, :], cols // LANES)),
    )
    send(out_ref, peak_ref[...] + shift + jnp.log2(total))

    @pl.when(jnp.logical_not(smallest(total)[0, 0] >= SAFE))
    def _():
        stand(standing, potential)
        for start in range(0, cols, TILE):
            part = score(source_ref[...], half_ref[start : start + TILE, :], scale) + spread(
                standing[...], TILE // LANES
            )
            peak = jnp.max(part, axis=0, keepdims=True)
            result = peak + jnp.log2(jnp.sum(jnp.exp2(part - peak), axis=0, keepdims=True))
            for lane in range(0, TILE, LANES):
                t = (start + lane) // LANES
                folded[t : t + 1, :] = result[:, lane : lane + LANES]
        send(out_ref, folded[...])


def finish(unit, row_bits, col_bits, row_parts_ref, column_parts_ref, row_ref, column_ref):
    row_ref[...] = unit * (col_bits - combine(row_parts_ref[...]))
    column_ref[...] = unit * (row_bits - combine(column_parts_ref[...]))


def local(source, target):
    f32 = jnp.float32
    own, width = source.shape
    plane = lax.axis_size(PLANE)
    line = lax.axis_size(LINE)
    cores = lax.axis_size("core")
    alike = lax.axis_size(ALIKE) if ALIKE else 1
    rows = own * cores * alike
    cols = target.shape[0] // cores
    row_bits = math.log2(rows * plane)
    col_bits = math.log2(cols * line)
    scale = math.log2(math.e) / (math.sqrt(width) * EPSILON)
    unit = EPSILON * math.log(2.0)
    core = lax.axis_index("core")
    swap = [(0, 1), (1, 0)]
    vmem = pl.BlockSpec(memory_space=pltpu.VMEM)
    hbm = pl.BlockSpec(memory_space=pltpu.HBM)
    row_shape = (rows // LANES, LANES)
    col_shape = (cols // LANES, LANES)
    limit = pltpu.CompilerParams(vmem_limit_bytes=32 * 2**20)

    parts, mine, half = pl.pallas_call(
        lambda *refs: first_rows(scale, *refs),
        in_specs=[hbm, hbm],
        out_specs=[vmem, vmem, vmem],
        out_shape=[
            jax.ShapeDtypeStruct((alike * line, own // LANES, LANES), f32),
            jax.ShapeDtypeStruct((own, width), f32),
            jax.ShapeDtypeStruct((cols, width), target.dtype),
        ],
        scratch_shapes=[
            pltpu.VMEM(source.shape, source.dtype),
            pltpu.VMEM((cols, width), target.dtype),
            pltpu.VMEM((own, target.shape[0]), f32),
            pltpu.VMEM((own, LANES), f32),
            pltpu.VMEM((own // LANES, LANES), f32),
            pltpu.SemaphoreType.DMA((2 * CHUNKS + 1,)),
        ],
        compiler_params=pltpu.CompilerParams(vmem_limit_bytes=52 * 2**20),
        name="first_rows",
    )(source, target)
    pieces = [mine]
    if ALIKE:
        pieces.append(lax.ppermute(mine, ALIKE, swap))
    pieces = [form for piece in pieces for form in (piece, lax.ppermute(piece, "core", swap))]
    gathered = lax.all_to_all(parts, ALIKE + LINE, 0, 0)
    parts, plan, row_base, peaks, source = pl.pallas_call(
        lambda *refs: first_columns(scale, col_bits, line // cores, *refs),
        in_specs=[vmem] * (len(pieces) + 2),
        out_specs=[vmem] * 5,
        out_shape=[
            jax.ShapeDtypeStruct((plane,) + col_shape, f32),
            jax.ShapeDtypeStruct((rows, cols), f32),
            jax.ShapeDtypeStruct(row_shape, f32),
            jax.ShapeDtypeStruct(col_shape, f32),
            jax.ShapeDtypeStruct((rows, width), source.dtype),
        ],
        scratch_shapes=[pltpu.VMEM((rows, LANES), f32), pltpu.VMEM(col_shape, f32)],
        compiler_params=limit,
        name="first_columns",
    )(*pieces, half, gathered)
    columns = lax.all_to_all(parts, PLANE, 0, 0)

    for step in range(1, ITERS):
        parts = pl.pallas_call(
            lambda *refs: later_rows(scale, row_bits, *refs),
            in_specs=[vmem] * 6,
            out_specs=vmem,
            out_shape=jax.ShapeDtypeStruct((line,) + row_shape, f32),
            scratch_shapes=[pltpu.VMEM(col_shape, f32), pltpu.VMEM(row_shape, f32)],
            compiler_params=limit,
            name="later_rows",
        )(columns, plan, row_base, peaks, source, half)
        gathered = lax.all_to_all(parts, LINE, 0, 0)
        parts = pl.pallas_call(
            lambda *refs: later_columns(scale, col_bits, *refs),
            in_specs=[vmem] * 6,
            out_specs=vmem,
            out_shape=jax.ShapeDtypeStruct((plane,) + col_shape, f32),
            scratch_shapes=[pltpu.VMEM((rows, LANES), f32), pltpu.VMEM(col_shape, f32)],
            compiler_params=limit,
            name="later_columns",
        )(gathered, plan, row_base, peaks, source, half)
        columns = lax.all_to_all(parts, PLANE, 0, 0)

    row_potential, column_potential = pl.pallas_call(
        lambda *refs: finish(unit, row_bits, col_bits, *refs),
        in_specs=[vmem] * 2,
        out_specs=[vmem] * 2,
        out_shape=[jax.ShapeDtypeStruct(row_shape, f32), jax.ShapeDtypeStruct(col_shape, f32)],
        compiler_params=limit,
        name="finish",
    )(gathered, columns)
    column_potential = column_potential.reshape(cols)
    other = lax.ppermute(column_potential, "core", swap)
    column_potential = jnp.where(
        core == 0,
        jnp.concatenate([column_potential, other]),
        jnp.concatenate([other, column_potential]),
    )
    start = lax.axis_index(ALIKE + ("core",)) * own
    row_potential = lax.dynamic_slice(row_potential.reshape(rows), (start,), (own,))
    return (row_potential, column_potential)


def solution(mesh):
    fine = Mesh(mesh.devices.reshape(8, 2, 2, 2, 4), ("z", "p", "q", "core", "x"))
    return jax.shard_map(
        local,
        mesh=fine,
        in_specs=(P(("z", "p", "q", "core"), None), P("x", None)),
        out_specs=(P(("z", "p", "q", "core")), P("x")),
        check_vma=False,
    )
```

```python
import math

import jax
import jax.numpy as jnp
from jax import lax
from jax.experimental import pallas as pl
from jax.experimental.pallas import tpu as pltpu
from jax.sharding import Mesh, PartitionSpec as P

ITERS = 4
EPSILON = 0.1
TILE = 256
LANES = 128
SUBLANES = 8
CHUNKS = 2
SAFE = 2.0**-80

FIRST_PLANE = ("z", "p", "q")
PLANE = ("z", "q")
LINE = ("core", "x")


def combine(parts):
    peak = jnp.max(parts, axis=0)
    return peak + jnp.log2(jnp.sum(jnp.exp2(parts - peak[None]), axis=0))


def largest(values):
    return jnp.max(jnp.max(values, axis=1, keepdims=True), axis=0, keepdims=True)


def smallest(values):
    return jnp.min(jnp.min(values, axis=1, keepdims=True), axis=0, keepdims=True)


def stand(ref, values):
    for k in range(values.shape[0]):
        ref[k * LANES : (k + 1) * LANES, :] = jnp.broadcast_to(values[k : k + 1], (LANES, LANES)).T


def fold(ref, row):
    for k in range(ref.shape[0]):
        ref[k : k + 1, :] = row[:, k * LANES : (k + 1) * LANES]
    return ref[...]


def spread(row, count):
    return jnp.concatenate([row] * count, axis=1)


def send(out_ref, values):
    for slot in range(out_ref.shape[0]):
        out_ref[slot] = values


def score(source, target, scale):
    return scale * lax.dot_general(
        source, target, (((1,), (1,)), ((), ())), preferred_element_type=jnp.float32
    )


def first_rows(
    scale, source_ref, target_ref, out_ref, wide_ref, half_ref, source, rest, scores, peaks, line, arrived
):
    core = lax.axis_index("core")
    rows, half = source.shape[0], half_ref.shape[0]
    chunk = half // CHUNKS
    fetch = pltpu.make_async_copy(source_ref, source, arrived.at[2 * CHUNKS])
    fetch.start()
    copies = []
    for side, place in ((core, half_ref), (1 - core, rest)):
        for k in range(CHUNKS):
            copies.append(
                pltpu.make_async_copy(
                    target_ref.at[pl.ds(pl.multiple_of(side * half + k * chunk, chunk), chunk)],
                    place.at[pl.ds(k * chunk, chunk)],
                    arrived.at[len(copies)],
                )
            )
            copies[-1].start()
    fetch.wait()
    wide_ref[...] = source[...].astype(jnp.float32)
    for start in range(0, 2 * half, TILE):
        if start % chunk == 0:
            copies[start // chunk].wait()
        place = half_ref if start < half else rest
        tile = slice(start, start + TILE)
        part = score(source[...], place[start % half : start % half + TILE, :], scale)
        scores[:, tile] = part
        high = part[:, :LANES]
        for lane in range(LANES, TILE, LANES):
            high = jnp.maximum(high, part[:, lane : lane + LANES])
        peaks[...] = high if start == 0 else jnp.maximum(peaks[...], high)
    for k in range(rows // LANES):
        block = slice(k * LANES, (k + 1) * LANES)
        peak = jnp.max(peaks[block, :], axis=1, keepdims=True)
        total = jnp.sum(jnp.exp2(scores[block, :] - peak), axis=1, keepdims=True)
        line[k : k + 1, :] = jnp.broadcast_to(peak + jnp.log2(total), (LANES, LANES)).T[:1]
    send(out_ref, line[...])


def column_sums(rows, width, get):
    total = lax.fori_loop(
        0,
        rows // SUBLANES,
        lambda k, total: total + get(pl.ds(pl.multiple_of(k * SUBLANES, SUBLANES), SUBLANES)),
        jnp.zeros((SUBLANES, width), jnp.float32),
        unroll=16,
    )
    return jnp.sum(total, axis=0, keepdims=True)


def place(source_ref, mine_ref, other_ref):
    core = lax.axis_index("core")
    own = mine_ref.shape[0]
    for side, piece in ((core, mine_ref), (1 - core, other_ref)):
        source_ref[pl.ds(pl.multiple_of(side * own, own), own), :] = piece[...].astype(source_ref.dtype)


def exponentials(scale, source_ref, half_ref, plan_ref, standing):
    rows, cols = plan_ref.shape
    highs = []
    for start in range(0, cols, TILE):
        tile = slice(start, start + TILE)
        part = score(source_ref[...], half_ref[tile, :], scale)
        if standing is not None:
            part = part + spread(standing[...], TILE // LANES)
        plan_ref[:, tile] = part
        highs.append(jnp.max(part, axis=0, keepdims=True))
    peak = jnp.concatenate(highs, axis=1)
    shift = jnp.broadcast_to(peak, (SUBLANES, cols))

    def term(block):
        value = jnp.exp2(plan_ref[block, :] - shift)
        plan_ref[block, :] = value
        return value

    return peak, column_sums(rows, cols, term)


def first_potential(bits, gathered_ref, away_ref, potential_ref, passed_ref):
    passed_ref[...] = away_ref[...]
    parts = gathered_ref[...]
    each = parts.shape[0] // 2
    potential_ref[...] = bits - jnp.concatenate([combine(parts[:each]), combine(parts[each:])], axis=0)


def first_columns(
    scale,
    mine_ref,
    other_ref,
    half_ref,
    potential_ref,
    out_ref,
    plan_ref,
    row_ref,
    peak_ref,
    source_ref,
    standing,
    folded,
):
    place(source_ref, mine_ref, other_ref)
    row_ref[...] = potential_ref[...]
    stand(standing, potential_ref[...])
    peak, total = exponentials(scale, source_ref, half_ref, plan_ref, standing)
    out_ref[...] = fold(peak_ref, peak) + jnp.log2(fold(folded, total))


def partner_rows(
    scale, mine_ref, other_ref, half_ref, columns_ref, out_ref, plan_ref, row_ref, peak_ref, source_ref
):
    send(out_ref, columns_ref[...])
    place(source_ref, mine_ref, other_ref)
    row_ref[...] = jnp.zeros_like(row_ref)
    peak, _ = exponentials(scale, source_ref, half_ref, plan_ref, None)
    fold(peak_ref, peak)


def later_rows(scale, bits, gathered_ref, half_ref, *refs):
    blocks, (out_ref, factor, totals) = (refs[:4], refs[4:8]), refs[8:]
    potential = bits - combine(gathered_ref[...])
    low = None
    for index, (plan_ref, row_ref, peak_ref, _) in enumerate(blocks):
        rows, cols = plan_ref.shape
        first = index * rows // LANES
        change = potential + peak_ref[...]
        shift = largest(change)
        factor[...] = jnp.exp2(change - shift)
        for k in range(rows // LANES):
            block = slice(k * LANES, (k + 1) * LANES)
            total = jnp.zeros((LANES, LANES), jnp.float32)
            for t in range(cols // LANES):
                total = total + plan_ref[block, t * LANES : (t + 1) * LANES] * factor[t : t + 1, :]
            totals[first + k : first + k + 1, :] = jnp.sum(total.T, axis=0, keepdims=True)
        part = slice(first, first + rows // LANES)
        total = totals[part, :]
        low = total if low is None else jnp.minimum(low, total)
        totals[part, :] = shift - row_ref[...] + jnp.log2(total)
    send(out_ref, totals[...])

    @pl.when(jnp.logical_not(smallest(low)[0, 0] >= SAFE))
    def _():
        wide = jnp.concatenate([potential[t : t + 1] for t in range(potential.shape[0])], axis=1)
        for index, (plan_ref, _, _, source_ref) in enumerate(blocks):
            count = plan_ref.shape[0] // LANES
            for k in range(count):
                part = score(source_ref[k * LANES : (k + 1) * LANES, :], half_ref[...], scale) + wide
                peak = jnp.max(part, axis=1, keepdims=True)
                total = jnp.sum(jnp.exp2(part - peak), axis=1, keepdims=True)
                row = index * count + k
                totals[row : row + 1, :] = jnp.broadcast_to(peak + jnp.log2(total), (LANES, LANES)).T[:1]
        send(out_ref, totals[...])


def later_columns(scale, bits, gathered_ref, half_ref, *refs):
    blocks, (out_ref, standing, folded) = (refs[:4], refs[4:8]), refs[8:]
    potential = bits - combine(gathered_ref[...])
    low = None
    results = []
    for index, (plan_ref, row_ref, peak_ref, _) in enumerate(blocks):
        rows, cols = plan_ref.shape
        count = cols // LANES
        change = potential[index * rows // LANES : (index + 1) * rows // LANES] - row_ref[...]
        shift = largest(change)
        stand(standing, jnp.exp2(change - shift))
        total = column_sums(rows, cols, lambda block: plan_ref[block, :] * spread(standing[block, :], count))
        total = fold(folded, total)
        low = total if low is None else jnp.minimum(low, total)
        results.append(peak_ref[...] + shift + jnp.log2(total))
    send(out_ref, combine(jnp.stack(results)))

    @pl.when(jnp.logical_not(smallest(low)[0, 0] >= SAFE))
    def _():
        for start in range(0, half_ref.shape[0], TILE):
            results = []
            for index, (plan_ref, _, _, source_ref) in enumerate(blocks):
                rows = plan_ref.shape[0]
                stand(standing, potential[index * rows // LANES : (index + 1) * rows // LANES])
                part = score(source_ref[...], half_ref[start : start + TILE, :], scale) + spread(
                    standing[...], TILE // LANES
                )
                peak = jnp.max(part, axis=0, keepdims=True)
                results.append(peak + jnp.log2(jnp.sum(jnp.exp2(part - peak), axis=0, keepdims=True)))
            result = combine(jnp.stack(results))
            for lane in range(0, TILE, LANES):
                t = (start + lane) // LANES
                folded[t : t + 1, :] = result[:, lane : lane + LANES]
        send(out_ref, folded[...])


def finish(unit, row_bits, col_bits, row_parts_ref, column_parts_ref, row_ref, column_ref):
    row_ref[...] = unit * (col_bits - combine(row_parts_ref[...]))
    column_ref[...] = unit * (row_bits - combine(column_parts_ref[...]))


def local(source, target):
    f32 = jnp.float32
    own, width = source.shape
    first_plane = lax.axis_size(FIRST_PLANE)
    plane = lax.axis_size(PLANE)
    line = lax.axis_size(LINE)
    cores = lax.axis_size("core")
    rows = own * cores
    cols = target.shape[0] // cores
    row_bits = math.log2(rows * first_plane)
    col_bits = math.log2(cols * line)
    scale = math.log2(math.e) / (math.sqrt(width) * EPSILON)
    unit = EPSILON * math.log(2.0)
    core = lax.axis_index("core")
    swap = [(0, 1), (1, 0)]
    vmem = pl.BlockSpec(memory_space=pltpu.VMEM)
    hbm = pl.BlockSpec(memory_space=pltpu.HBM)
    chip_shape = (rows // LANES, LANES)
    row_shape = (2 * rows // LANES, LANES)
    col_shape = (cols // LANES, LANES)
    limit = pltpu.CompilerParams(vmem_limit_bytes=24 * 2**20)
    block_out = [
        jax.ShapeDtypeStruct((rows, cols), f32),
        jax.ShapeDtypeStruct(chip_shape, f32),
        jax.ShapeDtypeStruct(col_shape, f32),
        jax.ShapeDtypeStruct((rows, width), source.dtype),
    ]

    parts, mine, half = pl.pallas_call(
        lambda *refs: first_rows(scale, *refs),
        in_specs=[hbm, hbm],
        out_specs=[vmem] * 3,
        out_shape=[
            jax.ShapeDtypeStruct((line, own // LANES, LANES), f32),
            jax.ShapeDtypeStruct((own, width), f32),
            jax.ShapeDtypeStruct((cols, width), target.dtype),
        ],
        scratch_shapes=[
            pltpu.VMEM(source.shape, source.dtype),
            pltpu.VMEM((cols, width), target.dtype),
            pltpu.VMEM((own, target.shape[0]), f32),
            pltpu.VMEM((own, LANES), f32),
            pltpu.VMEM((own // LANES, LANES), f32),
            pltpu.SemaphoreType.DMA((2 * CHUNKS + 1,)),
        ],
        compiler_params=pltpu.CompilerParams(vmem_limit_bytes=52 * 2**20),
        name="first_rows",
    )(source, target)
    other = lax.ppermute(mine, "core", swap)
    away = lax.ppermute(mine, ("p", "q"), [(0, 3), (3, 0), (1, 2), (2, 1)])
    gathered = lax.all_to_all(parts, LINE, 0, 0)
    potential, away = pl.pallas_call(
        lambda *refs: first_potential(col_bits, *refs),
        in_specs=[vmem] * 2,
        out_specs=[vmem] * 2,
        out_shape=[jax.ShapeDtypeStruct(chip_shape, f32), jax.ShapeDtypeStruct((own, width), f32)],
        compiler_params=limit,
        name="first_potential",
    )(gathered, away)
    columns, *mine_block = pl.pallas_call(
        lambda *refs: first_columns(scale, *refs),
        in_specs=[vmem] * 4,
        out_specs=[vmem] * 5,
        out_shape=[jax.ShapeDtypeStruct(col_shape, f32)] + block_out,
        scratch_shapes=[pltpu.VMEM((rows, LANES), f32), pltpu.VMEM(col_shape, f32)],
        compiler_params=limit,
        name="first_columns",
    )(mine, other, half, potential)
    parts, *away_block = pl.pallas_call(
        lambda *refs: partner_rows(scale, *refs),
        in_specs=[vmem] * 4,
        out_specs=[vmem] * 5,
        out_shape=[jax.ShapeDtypeStruct((first_plane,) + col_shape, f32)] + block_out,
        compiler_params=limit,
        name="partner_rows",
    )(away, lax.ppermute(away, "core", swap), half, columns)
    columns = lax.all_to_all(parts, FIRST_PLANE, 0, 0)

    for step in range(1, ITERS):
        parts = pl.pallas_call(
            lambda *refs: later_rows(scale, row_bits, *refs),
            in_specs=[vmem] * 10,
            out_specs=vmem,
            out_shape=jax.ShapeDtypeStruct((line,) + row_shape, f32),
            scratch_shapes=[pltpu.VMEM(col_shape, f32), pltpu.VMEM(row_shape, f32)],
            compiler_params=limit,
            name="later_rows",
        )(columns, half, *mine_block, *away_block)
        gathered = lax.all_to_all(parts, LINE, 0, 0)
        parts = pl.pallas_call(
            lambda *refs: later_columns(scale, col_bits, *refs),
            in_specs=[vmem] * 10,
            out_specs=vmem,
            out_shape=jax.ShapeDtypeStruct((plane,) + col_shape, f32),
            scratch_shapes=[pltpu.VMEM((rows, LANES), f32), pltpu.VMEM(col_shape, f32)],
            compiler_params=limit,
            name="later_columns",
        )(gathered, half, *mine_block, *away_block)
        columns = lax.all_to_all(parts, PLANE, 0, 0)

    row_potential, column_potential = pl.pallas_call(
        lambda *refs: finish(unit, row_bits, col_bits, *refs),
        in_specs=[vmem] * 2,
        out_specs=[vmem] * 2,
        out_shape=[jax.ShapeDtypeStruct(row_shape, f32), jax.ShapeDtypeStruct(col_shape, f32)],
        compiler_params=limit,
        name="finish",
    )(gathered, columns)
    column_potential = column_potential.reshape(cols)
    other = lax.ppermute(column_potential, "core", swap)
    column_potential = jnp.where(
        core == 0,
        jnp.concatenate([column_potential, other]),
        jnp.concatenate([other, column_potential]),
    )
    row_potential = lax.dynamic_slice(row_potential.reshape(2 * rows), (core * own,), (own,))
    return (row_potential, column_potential)


def solution(mesh):
    fine = Mesh(mesh.devices.reshape(8, 2, 2, 2, 4), ("z", "p", "q", "core", "x"))
    return jax.shard_map(
        local,
        mesh=fine,
        in_specs=(P(("z", "p", "q", "core"), None), P("x", None)),
        out_specs=(P(("z", "p", "q", "core")), P("x")),
        check_vma=False,
    )
```

```python
import math

import jax
import jax.numpy as jnp
from jax import lax
from jax.experimental import pallas as pl
from jax.experimental.pallas import tpu as pltpu
from jax.sharding import Mesh, PartitionSpec as P

ITERS = 4
EPSILON = 0.1
TILE = 256
LANES = 128
SUBLANES = 8
SAFE = 2.0**-80

FIRST_PLANE = ("z", "p", "q")
PLANE = ("z", "q")
LINE = ("core", "x")


def combine(parts):
    peak = jnp.max(parts, axis=0)
    return peak + jnp.log2(jnp.sum(jnp.exp2(parts - peak[None]), axis=0))


def largest(values):
    return jnp.max(jnp.max(values, axis=1, keepdims=True), axis=0, keepdims=True)


def smallest(values):
    return jnp.min(jnp.min(values, axis=1, keepdims=True), axis=0, keepdims=True)


def stand(ref, values):
    for k in range(values.shape[0]):
        ref[k * LANES : (k + 1) * LANES, :] = jnp.broadcast_to(values[k : k + 1], (LANES, LANES)).T


def fold(ref, row):
    for k in range(ref.shape[0]):
        ref[k : k + 1, :] = row[:, k * LANES : (k + 1) * LANES]
    return ref[...]


def spread(row, count):
    return jnp.concatenate([row] * count, axis=1)


def send(out_ref, values):
    for slot in range(out_ref.shape[0]):
        out_ref[slot] = values


def score(source, target, scale):
    return scale * lax.dot_general(
        source, target, (((1,), (1,)), ((), ())), preferred_element_type=jnp.float32
    )


def fetch(target_ref, half_ref, rest_ref, arrived):
    core = lax.axis_index("core")
    half = half_ref.shape[0]
    copies = [
        pltpu.make_async_copy(target_ref.at[pl.ds(pl.multiple_of(side * half, half), half)], place, arrived.at[k])
        for k, (side, place) in enumerate(((core, half_ref), (1 - core, rest_ref)))
    ]
    for copy in copies:
        copy.start()
    for copy in copies:
        copy.wait()


def first_rows(scale, source_ref, half_ref, rest_ref, out_ref, wide_ref, scores, peaks, line):
    rows, half = source_ref.shape[0], half_ref.shape[0]
    wide_ref[...] = source_ref[...].astype(jnp.float32)
    for start in range(0, 2 * half, TILE):
        place = half_ref if start < half else rest_ref
        tile = slice(start, start + TILE)
        part = score(source_ref[...], place[start % half : start % half + TILE, :], scale)
        scores[:, tile] = part
        high = part[:, :LANES]
        for lane in range(LANES, TILE, LANES):
            high = jnp.maximum(high, part[:, lane : lane + LANES])
        peaks[...] = high if start == 0 else jnp.maximum(peaks[...], high)
    for k in range(rows // LANES):
        block = slice(k * LANES, (k + 1) * LANES)
        peak = jnp.max(peaks[block, :], axis=1, keepdims=True)
        total = jnp.sum(jnp.exp2(scores[block, :] - peak), axis=1, keepdims=True)
        line[k : k + 1, :] = jnp.broadcast_to(peak + jnp.log2(total), (LANES, LANES)).T[:1]
    send(out_ref, line[...])


def column_sums(rows, width, get):
    total = lax.fori_loop(
        0,
        rows // SUBLANES,
        lambda k, total: total + get(pl.ds(pl.multiple_of(k * SUBLANES, SUBLANES), SUBLANES)),
        jnp.zeros((SUBLANES, width), jnp.float32),
        unroll=16,
    )
    return jnp.sum(total, axis=0, keepdims=True)


def place(source_ref, mine_ref, other_ref):
    core = lax.axis_index("core")
    own = mine_ref.shape[0]
    for side, piece in ((core, mine_ref), (1 - core, other_ref)):
        source_ref[pl.ds(pl.multiple_of(side * own, own), own), :] = piece[...].astype(source_ref.dtype)


def exponentials(scale, source_ref, half_ref, plan_ref, standing):
    rows, cols = plan_ref.shape
    highs = []
    for start in range(0, cols, TILE):
        tile = slice(start, start + TILE)
        part = score(source_ref[...], half_ref[tile, :], scale)
        if standing is not None:
            part = part + spread(standing[...], TILE // LANES)
        plan_ref[:, tile] = part
        highs.append(jnp.max(part, axis=0, keepdims=True))
    peak = jnp.concatenate(highs, axis=1)
    shift = jnp.broadcast_to(peak, (SUBLANES, cols))

    def term(block):
        value = jnp.exp2(plan_ref[block, :] - shift)
        plan_ref[block, :] = value
        return value

    return peak, column_sums(rows, cols, term)


def first_potential(bits, gathered_ref, away_ref, potential_ref, passed_ref):
    passed_ref[...] = away_ref[...]
    parts = gathered_ref[...]
    each = parts.shape[0] // 2
    potential_ref[...] = bits - jnp.concatenate([combine(parts[:each]), combine(parts[each:])], axis=0)


def first_columns(
    scale,
    mine_ref,
    other_ref,
    half_ref,
    potential_ref,
    out_ref,
    plan_ref,
    row_ref,
    peak_ref,
    source_ref,
    standing,
    folded,
):
    place(source_ref, mine_ref, other_ref)
    row_ref[...] = potential_ref[...]
    stand(standing, potential_ref[...])
    peak, total = exponentials(scale, source_ref, half_ref, plan_ref, standing)
    out_ref[...] = fold(peak_ref, peak) + jnp.log2(fold(folded, total))


def partner_rows(
    scale, mine_ref, other_ref, half_ref, plan_ref, row_ref, peak_ref, source_ref
):
    place(source_ref, mine_ref, other_ref)
    row_ref[...] = jnp.zeros_like(row_ref)
    peak, _ = exponentials(scale, source_ref, half_ref, plan_ref, None)
    fold(peak_ref, peak)


def later_rows(scale, bits, gathered_ref, half_ref, *refs):
    blocks, (out_ref, factor, totals) = (refs[:4], refs[4:8]), refs[8:]
    potential = bits - combine(gathered_ref[...])
    low = None
    for index, (plan_ref, row_ref, peak_ref, _) in enumerate(blocks):
        rows, cols = plan_ref.shape
        first = index * rows // LANES
        change = potential + peak_ref[...]
        shift = largest(change)
        factor[...] = jnp.exp2(change - shift)
        for k in range(rows // LANES):
            block = slice(k * LANES, (k + 1) * LANES)
            total = jnp.zeros((LANES, LANES), jnp.float32)
            for t in range(cols // LANES):
                total = total + plan_ref[block, t * LANES : (t + 1) * LANES] * factor[t : t + 1, :]
            totals[first + k : first + k + 1, :] = jnp.sum(total.T, axis=0, keepdims=True)
        part = slice(first, first + rows // LANES)
        total = totals[part, :]
        low = total if low is None else jnp.minimum(low, total)
        totals[part, :] = shift - row_ref[...] + jnp.log2(total)
    send(out_ref, totals[...])

    @pl.when(jnp.logical_not(smallest(low)[0, 0] >= SAFE))
    def _():
        wide = jnp.concatenate([potential[t : t + 1] for t in range(potential.shape[0])], axis=1)
        for index, (plan_ref, _, _, source_ref) in enumerate(blocks):
            count = plan_ref.shape[0] // LANES
            for k in range(count):
                part = score(source_ref[k * LANES : (k + 1) * LANES, :], half_ref[...], scale) + wide
                peak = jnp.max(part, axis=1, keepdims=True)
                total = jnp.sum(jnp.exp2(part - peak), axis=1, keepdims=True)
                row = index * count + k
                totals[row : row + 1, :] = jnp.broadcast_to(peak + jnp.log2(total), (LANES, LANES)).T[:1]
        send(out_ref, totals[...])


def scaled_columns(scale, potential, start_from, half_ref, blocks, out_ref, standing, folded):
    rows, cols = blocks[0][0].shape
    count = rows // LANES
    low = None
    results = list(start_from)
    for index, (plan_ref, row_ref, peak_ref, _) in enumerate(blocks):
        change = potential[index * count : (index + 1) * count] - row_ref[...]
        shift = largest(change)
        stand(standing, jnp.exp2(change - shift))
        total = column_sums(
            rows, cols, lambda block: plan_ref[block, :] * spread(standing[block, :], cols // LANES)
        )
        total = fold(folded, total)
        low = total if low is None else jnp.minimum(low, total)
        results.append(peak_ref[...] + shift + jnp.log2(total))
    send(out_ref, combine(jnp.stack(results)))

    @pl.when(jnp.logical_not(smallest(low)[0, 0] >= SAFE))
    def _():
        for start in range(0, cols, TILE):
            results = []
            for index, (_, _, _, source_ref) in enumerate(blocks):
                stand(standing, potential[index * count : (index + 1) * count])
                part = score(source_ref[...], half_ref[start : start + TILE, :], scale) + spread(
                    standing[...], TILE // LANES
                )
                peak = jnp.max(part, axis=0, keepdims=True)
                results.append(peak + jnp.log2(jnp.sum(jnp.exp2(part - peak), axis=0, keepdims=True)))
            result = combine(jnp.stack(results))
            for lane in range(0, TILE, LANES):
                t = (start + lane) // LANES
                folded[t : t + 1, :] = result[:, lane : lane + LANES]
        send(out_ref, combine(jnp.stack(list(start_from) + [folded[...]])))


def partner_columns(scale, columns_ref, potential_ref, half_ref, *refs):
    scaled_columns(scale, potential_ref[...], [columns_ref[...]], half_ref, (refs[:4],), *refs[4:])


def later_columns(scale, bits, gathered_ref, half_ref, *refs):
    potential = bits - combine(gathered_ref[...])
    scaled_columns(scale, potential, [], half_ref, (refs[:4], refs[4:8]), *refs[8:])


def finish(unit, row_bits, col_bits, row_parts_ref, column_parts_ref, row_ref, column_ref):
    row_ref[...] = unit * (col_bits - combine(row_parts_ref[...]))
    column_ref[...] = unit * (row_bits - combine(column_parts_ref[...]))


def local(source, target):
    f32 = jnp.float32
    own, width = source.shape
    first_plane = lax.axis_size(FIRST_PLANE)
    plane = lax.axis_size(PLANE)
    line = lax.axis_size(LINE)
    cores = lax.axis_size("core")
    rows = own * cores
    cols = target.shape[0] // cores
    row_bits = math.log2(rows * first_plane)
    col_bits = math.log2(cols * line)
    scale = math.log2(math.e) / (math.sqrt(width) * EPSILON)
    unit = EPSILON * math.log(2.0)
    core = lax.axis_index("core")
    swap = [(0, 1), (1, 0)]
    partner = [(0, 3), (3, 0), (1, 2), (2, 1)]
    vmem = pl.BlockSpec(memory_space=pltpu.VMEM)
    hbm = pl.BlockSpec(memory_space=pltpu.HBM)
    chip_shape = (rows // LANES, LANES)
    row_shape = (2 * rows // LANES, LANES)
    col_shape = (cols // LANES, LANES)
    limit = pltpu.CompilerParams(vmem_limit_bytes=24 * 2**20)
    block_out = [
        jax.ShapeDtypeStruct((rows, cols), f32),
        jax.ShapeDtypeStruct(chip_shape, f32),
        jax.ShapeDtypeStruct(col_shape, f32),
        jax.ShapeDtypeStruct((rows, width), source.dtype),
    ]

    half, rest = pl.pallas_call(
        fetch,
        in_specs=[hbm],
        out_specs=[vmem] * 2,
        out_shape=[jax.ShapeDtypeStruct((cols, width), target.dtype)] * 2,
        scratch_shapes=[pltpu.SemaphoreType.DMA((2,))],
        compiler_params=pltpu.CompilerParams(vmem_limit_bytes=51 * 2**20),
        name="fetch",
    )(target)
    parts, mine = pl.pallas_call(
        lambda *refs: first_rows(scale, *refs),
        in_specs=[vmem] * 3,
        out_specs=[vmem] * 2,
        out_shape=[
            jax.ShapeDtypeStruct((line, own // LANES, LANES), f32),
            jax.ShapeDtypeStruct((own, width), f32),
        ],
        scratch_shapes=[
            pltpu.VMEM((own, target.shape[0]), f32),
            pltpu.VMEM((own, LANES), f32),
            pltpu.VMEM((own // LANES, LANES), f32),
        ],
        compiler_params=limit,
        name="first_rows",
    )(source, half, rest)
    other = lax.ppermute(mine, "core", swap)
    away = lax.ppermute(mine, ("p", "q"), partner)
    gathered = lax.all_to_all(parts, LINE, 0, 0)
    potential, away = pl.pallas_call(
        lambda *refs: first_potential(col_bits, *refs),
        in_specs=[vmem] * 2,
        out_specs=[vmem] * 2,
        out_shape=[jax.ShapeDtypeStruct(chip_shape, f32), jax.ShapeDtypeStruct((own, width), f32)],
        compiler_params=limit,
        name="first_potential",
    )(gathered, away)
    away_potential = lax.ppermute(potential, ("p", "q"), partner)
    columns, *mine_block = pl.pallas_call(
        lambda *refs: first_columns(scale, *refs),
        in_specs=[vmem] * 4,
        out_specs=[vmem] * 5,
        out_shape=[jax.ShapeDtypeStruct(col_shape, f32)] + block_out,
        scratch_shapes=[pltpu.VMEM((rows, LANES), f32), pltpu.VMEM(col_shape, f32)],
        compiler_params=limit,
        name="first_columns",
    )(mine, other, half, potential)
    away_block = pl.pallas_call(
        lambda *refs: partner_rows(scale, *refs),
        in_specs=[vmem] * 3,
        out_specs=[vmem] * 4,
        out_shape=block_out,
        compiler_params=limit,
        name="partner_rows",
    )(away, lax.ppermute(away, "core", swap), half)
    column_out = jax.ShapeDtypeStruct((plane,) + col_shape, f32)
    column_scratch = [pltpu.VMEM((rows, LANES), f32), pltpu.VMEM(col_shape, f32)]
    parts = pl.pallas_call(
        lambda *refs: partner_columns(scale, *refs),
        in_specs=[vmem] * 7,
        out_specs=vmem,
        out_shape=column_out,
        scratch_shapes=column_scratch,
        compiler_params=limit,
        name="partner_columns",
    )(columns, away_potential, half, *away_block)
    columns = lax.all_to_all(parts, PLANE, 0, 0)

    for step in range(1, ITERS):
        parts = pl.pallas_call(
            lambda *refs: later_rows(scale, row_bits, *refs),
            in_specs=[vmem] * 10,
            out_specs=vmem,
            out_shape=jax.ShapeDtypeStruct((line,) + row_shape, f32),
            scratch_shapes=[pltpu.VMEM(col_shape, f32), pltpu.VMEM(row_shape, f32)],
            compiler_params=limit,
            name="later_rows",
        )(columns, half, *mine_block, *away_block)
        gathered = lax.all_to_all(parts, LINE, 0, 0)
        parts = pl.pallas_call(
            lambda *refs: later_columns(scale, col_bits, *refs),
            in_specs=[vmem] * 10,
            out_specs=vmem,
            out_shape=column_out,
            scratch_shapes=column_scratch,
            compiler_params=limit,
            name="later_columns",
        )(gathered, half, *mine_block, *away_block)
        columns = lax.all_to_all(parts, PLANE, 0, 0)

    row_potential, column_potential = pl.pallas_call(
        lambda *refs: finish(unit, row_bits, col_bits, *refs),
        in_specs=[vmem] * 2,
        out_specs=[vmem] * 2,
        out_shape=[jax.ShapeDtypeStruct(row_shape, f32), jax.ShapeDtypeStruct(col_shape, f32)],
        compiler_params=limit,
        name="finish",
    )(gathered, columns)
    column_potential = column_potential.reshape(cols)
    other = lax.ppermute(column_potential, "core", swap)
    column_potential = jnp.where(
        core == 0,
        jnp.concatenate([column_potential, other]),
        jnp.concatenate([other, column_potential]),
    )
    row_potential = lax.dynamic_slice(row_potential.reshape(2 * rows), (core * own,), (own,))
    return (row_potential, column_potential)


def solution(mesh):
    fine = Mesh(mesh.devices.reshape(8, 2, 2, 2, 4), ("z", "p", "q", "core", "x"))
    return jax.shard_map(
        local,
        mesh=fine,
        in_specs=(P(("z", "p", "q", "core"), None), P("x", None)),
        out_specs=(P(("z", "p", "q", "core")), P("x")),
        check_vma=False,
    )
```

```python
import math

import jax
import jax.numpy as jnp
from jax import lax
from jax.experimental import pallas as pl
from jax.experimental.pallas import tpu as pltpu
from jax.sharding import Mesh, PartitionSpec as P

ITERS = 4
EPSILON = 0.1
TILE = 256
LANES = 128
SUBLANES = 8
SAFE = 2.0**-80

FIRST_PLANE = ("z", "p", "q")
PLANE = ("z", "q")
LINE = ("core", "x")


def combine(parts):
    peak = jnp.max(parts, axis=0)
    return peak + jnp.log2(jnp.sum(jnp.exp2(parts - peak[None]), axis=0))


def largest(values):
    return jnp.max(jnp.max(values, axis=1, keepdims=True), axis=0, keepdims=True)


def smallest(values):
    return jnp.min(jnp.min(values, axis=1, keepdims=True), axis=0, keepdims=True)


def stand(ref, values):
    for k in range(values.shape[0]):
        ref[k * LANES : (k + 1) * LANES, :] = jnp.broadcast_to(values[k : k + 1], (LANES, LANES)).T


def fold(ref, row):
    for k in range(ref.shape[0]):
        ref[k : k + 1, :] = row[:, k * LANES : (k + 1) * LANES]
    return ref[...]


def spread(row, count):
    return jnp.concatenate([row] * count, axis=1)


def send(out_ref, values):
    for slot in range(out_ref.shape[0]):
        out_ref[slot] = values


def score(source, target, scale):
    return scale * lax.dot_general(
        source, target, (((1,), (1,)), ((), ())), preferred_element_type=jnp.float32
    )


def fetch(target_ref, half_ref, rest_ref, arrived):
    core = lax.axis_index("core")
    half = half_ref.shape[0]
    copies = [
        pltpu.make_async_copy(target_ref.at[pl.ds(pl.multiple_of(side * half, half), half)], place, arrived.at[k])
        for k, (side, place) in enumerate(((core, half_ref), (1 - core, rest_ref)))
    ]
    for copy in copies:
        copy.start()
    for copy in copies:
        copy.wait()


def first_rows(scale, source_ref, half_ref, rest_ref, out_ref, wide_ref, scores, peaks, line):
    rows, half = source_ref.shape[0], half_ref.shape[0]
    wide_ref[...] = source_ref[...].astype(jnp.float32)
    for start in range(0, 2 * half, TILE):
        place = half_ref if start < half else rest_ref
        tile = slice(start, start + TILE)
        part = score(source_ref[...], place[start % half : start % half + TILE, :], scale)
        scores[:, tile] = part
        high = part[:, :LANES]
        for lane in range(LANES, TILE, LANES):
            high = jnp.maximum(high, part[:, lane : lane + LANES])
        peaks[...] = high if start == 0 else jnp.maximum(peaks[...], high)
    for k in range(rows // LANES):
        block = slice(k * LANES, (k + 1) * LANES)
        peak = jnp.max(peaks[block, :], axis=1, keepdims=True)
        total = jnp.sum(jnp.exp2(scores[block, :] - peak), axis=1, keepdims=True)
        line[k : k + 1, :] = jnp.broadcast_to(peak + jnp.log2(total), (LANES, LANES)).T[:1]
    send(out_ref, line[...])


def column_sums(rows, width, get):
    total = lax.fori_loop(
        0,
        rows // SUBLANES,
        lambda k, total: total + get(pl.ds(pl.multiple_of(k * SUBLANES, SUBLANES), SUBLANES)),
        jnp.zeros((SUBLANES, width), jnp.float32),
        unroll=64,
    )
    return jnp.sum(total, axis=0, keepdims=True)


def place(source_ref, mine_ref, other_ref):
    core = lax.axis_index("core")
    own = mine_ref.shape[0]
    for side, piece in ((core, mine_ref), (1 - core, other_ref)):
        source_ref[pl.ds(pl.multiple_of(side * own, own), own), :] = piece[...].astype(source_ref.dtype)


def exponentials(scale, source_ref, half_ref, plan_ref, standing):
    rows, cols = plan_ref.shape
    highs = []
    for start in range(0, cols, TILE):
        tile = slice(start, start + TILE)
        part = score(source_ref[...], half_ref[tile, :], scale)
        if standing is not None:
            part = part + spread(standing[...], TILE // LANES)
        plan_ref[:, tile] = part
        highs.append(jnp.max(part, axis=0, keepdims=True))
    peak = jnp.concatenate(highs, axis=1)
    shift = jnp.broadcast_to(peak, (SUBLANES, cols))

    def term(block):
        value = jnp.exp2(plan_ref[block, :] - shift)
        plan_ref[block, :] = value
        return value

    return peak, column_sums(rows, cols, term)


def first_potential(bits, gathered_ref, mine_ref, away_ref, potential_ref, mine_out, away_out):
    mine_out[...] = mine_ref[...]
    away_out[...] = away_ref[...]
    parts = gathered_ref[...]
    each = parts.shape[0] // 2
    potential_ref[...] = bits - jnp.concatenate([combine(parts[:each]), combine(parts[each:])], axis=0)


def first_columns(
    scale,
    mine_ref,
    other_ref,
    half_ref,
    potential_ref,
    out_ref,
    plan_ref,
    row_ref,
    peak_ref,
    source_ref,
    standing,
    folded,
):
    place(source_ref, mine_ref, other_ref)
    row_ref[...] = potential_ref[...]
    stand(standing, potential_ref[...])
    peak, total = exponentials(scale, source_ref, half_ref, plan_ref, standing)
    out_ref[...] = fold(peak_ref, peak) + jnp.log2(fold(folded, total))


def partner_rows(
    scale, mine_ref, other_ref, half_ref, plan_ref, row_ref, peak_ref, source_ref
):
    place(source_ref, mine_ref, other_ref)
    row_ref[...] = jnp.zeros_like(row_ref)
    peak, _ = exponentials(scale, source_ref, half_ref, plan_ref, None)
    fold(peak_ref, peak)


def later_rows(scale, bits, gathered_ref, half_ref, *refs):
    blocks, (out_ref, factor, totals) = (refs[:4], refs[4:8]), refs[8:]
    potential = bits - combine(gathered_ref[...])
    low = None
    for index, (plan_ref, row_ref, peak_ref, _) in enumerate(blocks):
        rows, cols = plan_ref.shape
        first = index * rows // LANES
        change = potential + peak_ref[...]
        shift = largest(change)
        factor[...] = jnp.exp2(change - shift)
        for k in range(rows // LANES):
            block = slice(k * LANES, (k + 1) * LANES)
            total = jnp.zeros((LANES, LANES), jnp.float32)
            for t in range(cols // LANES):
                total = total + plan_ref[block, t * LANES : (t + 1) * LANES] * factor[t : t + 1, :]
            totals[first + k : first + k + 1, :] = jnp.sum(total.T, axis=0, keepdims=True)
        part = slice(first, first + rows // LANES)
        total = totals[part, :]
        low = total if low is None else jnp.minimum(low, total)
        totals[part, :] = shift - row_ref[...] + jnp.log2(total)
    send(out_ref, totals[...])

    @pl.when(jnp.logical_not(smallest(low)[0, 0] >= SAFE))
    def _():
        wide = jnp.concatenate([potential[t : t + 1] for t in range(potential.shape[0])], axis=1)
        for index, (plan_ref, _, _, source_ref) in enumerate(blocks):
            count = plan_ref.shape[0] // LANES
            for k in range(count):
                part = score(source_ref[k * LANES : (k + 1) * LANES, :], half_ref[...], scale) + wide
                peak = jnp.max(part, axis=1, keepdims=True)
                total = jnp.sum(jnp.exp2(part - peak), axis=1, keepdims=True)
                row = index * count + k
                totals[row : row + 1, :] = jnp.broadcast_to(peak + jnp.log2(total), (LANES, LANES)).T[:1]
        send(out_ref, totals[...])


def scaled_columns(scale, potential, start_from, half_ref, blocks, out_ref, standing, folded):
    rows, cols = blocks[0][0].shape
    count = rows // LANES
    low = None
    results = list(start_from)
    for index, (plan_ref, row_ref, peak_ref, _) in enumerate(blocks):
        change = potential[index * count : (index + 1) * count] - row_ref[...]
        shift = largest(change)
        stand(standing, jnp.exp2(change - shift))
        total = column_sums(
            rows, cols, lambda block: plan_ref[block, :] * spread(standing[block, :], cols // LANES)
        )
        total = fold(folded, total)
        low = total if low is None else jnp.minimum(low, total)
        results.append(peak_ref[...] + shift + jnp.log2(total))
    send(out_ref, combine(jnp.stack(results)))

    @pl.when(jnp.logical_not(smallest(low)[0, 0] >= SAFE))
    def _():
        for start in range(0, cols, TILE):
            results = []
            for index, (_, _, _, source_ref) in enumerate(blocks):
                stand(standing, potential[index * count : (index + 1) * count])
                part = score(source_ref[...], half_ref[start : start + TILE, :], scale) + spread(
                    standing[...], TILE // LANES
                )
                peak = jnp.max(part, axis=0, keepdims=True)
                results.append(peak + jnp.log2(jnp.sum(jnp.exp2(part - peak), axis=0, keepdims=True)))
            result = combine(jnp.stack(results))
            for lane in range(0, TILE, LANES):
                t = (start + lane) // LANES
                folded[t : t + 1, :] = result[:, lane : lane + LANES]
        send(out_ref, combine(jnp.stack(list(start_from) + [folded[...]])))


def partner_columns(scale, columns_ref, potential_ref, half_ref, *refs):
    scaled_columns(scale, potential_ref[...], [columns_ref[...]], half_ref, (refs[:4],), *refs[4:])


def later_columns(scale, bits, gathered_ref, half_ref, *refs):
    potential = bits - combine(gathered_ref[...])
    scaled_columns(scale, potential, [], half_ref, (refs[:4], refs[4:8]), *refs[8:])


def finish(unit, row_bits, col_bits, row_parts_ref, column_parts_ref, row_ref, column_ref):
    row_ref[...] = unit * (col_bits - combine(row_parts_ref[...]))
    column_ref[...] = unit * (row_bits - combine(column_parts_ref[...]))


def local(source, target):
    f32 = jnp.float32
    own, width = source.shape
    first_plane = lax.axis_size(FIRST_PLANE)
    plane = lax.axis_size(PLANE)
    line = lax.axis_size(LINE)
    cores = lax.axis_size("core")
    rows = own * cores
    cols = target.shape[0] // cores
    row_bits = math.log2(rows * first_plane)
    col_bits = math.log2(cols * line)
    scale = math.log2(math.e) / (math.sqrt(width) * EPSILON)
    unit = EPSILON * math.log(2.0)
    core = lax.axis_index("core")
    swap = [(0, 1), (1, 0)]
    partner = [(0, 3), (3, 0), (1, 2), (2, 1)]
    vmem = pl.BlockSpec(memory_space=pltpu.VMEM)
    hbm = pl.BlockSpec(memory_space=pltpu.HBM)
    chip_shape = (rows // LANES, LANES)
    row_shape = (2 * rows // LANES, LANES)
    col_shape = (cols // LANES, LANES)
    limit = pltpu.CompilerParams(vmem_limit_bytes=24 * 2**20)
    block_out = [
        jax.ShapeDtypeStruct((rows, cols), f32),
        jax.ShapeDtypeStruct(chip_shape, f32),
        jax.ShapeDtypeStruct(col_shape, f32),
        jax.ShapeDtypeStruct((rows, width), source.dtype),
    ]

    half, rest = pl.pallas_call(
        fetch,
        in_specs=[hbm],
        out_specs=[vmem] * 2,
        out_shape=[jax.ShapeDtypeStruct((cols, width), target.dtype)] * 2,
        scratch_shapes=[pltpu.SemaphoreType.DMA((2,))],
        compiler_params=pltpu.CompilerParams(vmem_limit_bytes=51 * 2**20),
        name="fetch",
    )(target)
    parts, mine = pl.pallas_call(
        lambda *refs: first_rows(scale, *refs),
        in_specs=[vmem] * 3,
        out_specs=[vmem] * 2,
        out_shape=[
            jax.ShapeDtypeStruct((line, own // LANES, LANES), f32),
            jax.ShapeDtypeStruct((own, width), f32),
        ],
        scratch_shapes=[
            pltpu.VMEM((own, target.shape[0]), f32),
            pltpu.VMEM((own, LANES), f32),
            pltpu.VMEM((own // LANES, LANES), f32),
        ],
        compiler_params=limit,
        name="first_rows",
    )(source, half, rest)
    away = lax.ppermute(mine, ("p", "q"), partner)
    gathered = lax.all_to_all(parts, LINE, 0, 0)
    potential, mine, away = pl.pallas_call(
        lambda *refs: first_potential(col_bits, *refs),
        in_specs=[vmem] * 3,
        out_specs=[vmem] * 3,
        out_shape=[jax.ShapeDtypeStruct(chip_shape, f32)] + [jax.ShapeDtypeStruct((own, width), f32)] * 2,
        compiler_params=limit,
        name="first_potential",
    )(gathered, mine, away)
    other = lax.ppermute(mine, "core", swap)
    away_potential = lax.ppermute(potential, ("p", "q"), partner)
    columns, *mine_block = pl.pallas_call(
        lambda *refs: first_columns(scale, *refs),
        in_specs=[vmem] * 4,
        out_specs=[vmem] * 5,
        out_shape=[jax.ShapeDtypeStruct(col_shape, f32)] + block_out,
        scratch_shapes=[pltpu.VMEM((rows, LANES), f32), pltpu.VMEM(col_shape, f32)],
        compiler_params=limit,
        name="first_columns",
    )(mine, other, half, potential)
    away_block = pl.pallas_call(
        lambda *refs: partner_rows(scale, *refs),
        in_specs=[vmem] * 3,
        out_specs=[vmem] * 4,
        out_shape=block_out,
        compiler_params=limit,
        name="partner_rows",
    )(away, lax.ppermute(away, "core", swap), half)
    column_out = jax.ShapeDtypeStruct((plane,) + col_shape, f32)
    column_scratch = [pltpu.VMEM((rows, LANES), f32), pltpu.VMEM(col_shape, f32)]
    parts = pl.pallas_call(
        lambda *refs: partner_columns(scale, *refs),
        in_specs=[vmem] * 7,
        out_specs=vmem,
        out_shape=column_out,
        scratch_shapes=column_scratch,
        compiler_params=limit,
        name="partner_columns",
    )(columns, away_potential, half, *away_block)
    columns = lax.all_to_all(parts, PLANE, 0, 0)

    for step in range(1, ITERS):
        parts = pl.pallas_call(
            lambda *refs: later_rows(scale, row_bits, *refs),
            in_specs=[vmem] * 10,
            out_specs=vmem,
            out_shape=jax.ShapeDtypeStruct((line,) + row_shape, f32),
            scratch_shapes=[pltpu.VMEM(col_shape, f32), pltpu.VMEM(row_shape, f32)],
            compiler_params=limit,
            name="later_rows",
        )(columns, half, *mine_block, *away_block)
        gathered = lax.all_to_all(parts, LINE, 0, 0)
        parts = pl.pallas_call(
            lambda *refs: later_columns(scale, col_bits, *refs),
            in_specs=[vmem] * 10,
            out_specs=vmem,
            out_shape=column_out,
            scratch_shapes=column_scratch,
            compiler_params=limit,
            name="later_columns",
        )(gathered, half, *mine_block, *away_block)
        columns = lax.all_to_all(parts, PLANE, 0, 0)

    row_potential, column_potential = pl.pallas_call(
        lambda *refs: finish(unit, row_bits, col_bits, *refs),
        in_specs=[vmem] * 2,
        out_specs=[vmem] * 2,
        out_shape=[jax.ShapeDtypeStruct(row_shape, f32), jax.ShapeDtypeStruct(col_shape, f32)],
        compiler_params=limit,
        name="finish",
    )(gathered, columns)
    column_potential = column_potential.reshape(cols)
    other = lax.ppermute(column_potential, "core", swap)
    column_potential = jnp.where(
        core == 0,
        jnp.concatenate([column_potential, other]),
        jnp.concatenate([other, column_potential]),
    )
    row_potential = lax.dynamic_slice(row_potential.reshape(2 * rows), (core * own,), (own,))
    return (row_potential, column_potential)


def solution(mesh):
    fine = Mesh(mesh.devices.reshape(8, 2, 2, 2, 4), ("z", "p", "q", "core", "x"))
    return jax.shard_map(
        local,
        mesh=fine,
        in_specs=(P(("z", "p", "q", "core"), None), P("x", None)),
        out_specs=(P(("z", "p", "q", "core")), P("x")),
        check_vma=False,
    )
```

```python
import math

import jax
import jax.numpy as jnp
from jax import lax
from jax.experimental import pallas as pl
from jax.experimental.pallas import tpu as pltpu
from jax.sharding import Mesh, PartitionSpec as P

ITERS = 4
EPSILON = 0.1
TILE = 256
LANES = 128
SUBLANES = 8
SAFE = 2.0**-80

FIRST_PLANE = ("z", "p", "q")
PLANE = ("q", "z")
LINE = ("core", "x")


def combine(parts):
    peak = jnp.max(parts, axis=0)
    return peak + jnp.log2(jnp.sum(jnp.exp2(parts - peak[None]), axis=0))


def largest(values):
    return jnp.max(jnp.max(values, axis=1, keepdims=True), axis=0, keepdims=True)


def smallest(values):
    return jnp.min(jnp.min(values, axis=1, keepdims=True), axis=0, keepdims=True)


def stand(ref, values):
    for k in range(values.shape[0]):
        ref[k * LANES : (k + 1) * LANES, :] = jnp.broadcast_to(values[k : k + 1], (LANES, LANES)).T


def fold(ref, row):
    for k in range(ref.shape[0]):
        ref[k : k + 1, :] = row[:, k * LANES : (k + 1) * LANES]
    return ref[...]


def spread(row, count):
    return jnp.concatenate([row] * count, axis=1)


def send(out_ref, values):
    for slot in range(out_ref.shape[0]):
        out_ref[slot] = values


def score(source, target, scale):
    return scale * lax.dot_general(
        source, target, (((1,), (1,)), ((), ())), preferred_element_type=jnp.float32
    )


def fetch(target_ref, half_ref, rest_ref, arrived):
    core = lax.axis_index("core")
    half = half_ref.shape[0]
    copies = [
        pltpu.make_async_copy(target_ref.at[pl.ds(pl.multiple_of(side * half, half), half)], place, arrived.at[k])
        for k, (side, place) in enumerate(((core, half_ref), (1 - core, rest_ref)))
    ]
    for copy in copies:
        copy.start()
    for copy in copies:
        copy.wait()


def first_rows(scale, source_ref, half_ref, rest_ref, out_ref, wide_ref, scores, peaks, line):
    rows, half = source_ref.shape[0], half_ref.shape[0]
    wide_ref[...] = source_ref[...].astype(jnp.float32)
    for start in range(0, 2 * half, TILE):
        place = half_ref if start < half else rest_ref
        tile = slice(start, start + TILE)
        part = score(source_ref[...], place[start % half : start % half + TILE, :], scale)
        scores[:, tile] = part
        high = part[:, :LANES]
        for lane in range(LANES, TILE, LANES):
            high = jnp.maximum(high, part[:, lane : lane + LANES])
        peaks[...] = high if start == 0 else jnp.maximum(peaks[...], high)
    for k in range(rows // LANES):
        block = slice(k * LANES, (k + 1) * LANES)
        peak = jnp.max(peaks[block, :], axis=1, keepdims=True)
        total = jnp.sum(jnp.exp2(scores[block, :] - peak), axis=1, keepdims=True)
        line[k : k + 1, :] = jnp.broadcast_to(peak + jnp.log2(total), (LANES, LANES)).T[:1]
    send(out_ref, line[...])


def column_sums(rows, width, get):
    total = lax.fori_loop(
        0,
        rows // SUBLANES,
        lambda k, total: total + get(pl.ds(pl.multiple_of(k * SUBLANES, SUBLANES), SUBLANES)),
        jnp.zeros((SUBLANES, width), jnp.float32),
        unroll=64,
    )
    return jnp.sum(total, axis=0, keepdims=True)


def place(source_ref, mine_ref, other_ref):
    core = lax.axis_index("core")
    own = mine_ref.shape[0]
    for side, piece in ((core, mine_ref), (1 - core, other_ref)):
        source_ref[pl.ds(pl.multiple_of(side * own, own), own), :] = piece[...].astype(source_ref.dtype)


def exponentials(scale, source_ref, half_ref, plan_ref, standing):
    rows, cols = plan_ref.shape
    highs = []
    for start in range(0, cols, TILE):
        tile = slice(start, start + TILE)
        part = score(source_ref[...], half_ref[tile, :], scale)
        if standing is not None:
            part = part + spread(standing[...], TILE // LANES)
        plan_ref[:, tile] = part
        highs.append(jnp.max(part, axis=0, keepdims=True))
    peak = jnp.concatenate(highs, axis=1)
    shift = jnp.broadcast_to(peak, (SUBLANES, cols))

    def term(block):
        value = jnp.exp2(plan_ref[block, :] - shift)
        plan_ref[block, :] = value
        return value

    return peak, column_sums(rows, cols, term)


def first_potential(bits, gathered_ref, mine_ref, away_ref, potential_ref, mine_out, away_out):
    mine_out[...] = mine_ref[...]
    away_out[...] = away_ref[...]
    parts = gathered_ref[...]
    each = parts.shape[0] // 2
    potential_ref[...] = bits - jnp.concatenate([combine(parts[:each]), combine(parts[each:])], axis=0)


def first_columns(
    scale,
    mine_ref,
    other_ref,
    half_ref,
    potential_ref,
    out_ref,
    plan_ref,
    row_ref,
    peak_ref,
    source_ref,
    standing,
    folded,
):
    place(source_ref, mine_ref, other_ref)
    row_ref[...] = potential_ref[...]
    stand(standing, potential_ref[...])
    peak, total = exponentials(scale, source_ref, half_ref, plan_ref, standing)
    out_ref[...] = fold(peak_ref, peak) + jnp.log2(fold(folded, total))


def partner_rows(
    scale, mine_ref, other_ref, half_ref, plan_ref, row_ref, peak_ref, source_ref
):
    place(source_ref, mine_ref, other_ref)
    row_ref[...] = jnp.zeros_like(row_ref)
    peak, _ = exponentials(scale, source_ref, half_ref, plan_ref, None)
    fold(peak_ref, peak)


def later_rows(scale, bits, gathered_ref, half_ref, *refs):
    blocks, (out_ref, factor, totals) = (refs[:4], refs[4:8]), refs[8:]
    potential = bits - combine(gathered_ref[...])
    low = None
    for index, (plan_ref, row_ref, peak_ref, _) in enumerate(blocks):
        rows, cols = plan_ref.shape
        first = index * rows // LANES
        change = potential + peak_ref[...]
        shift = largest(change)
        factor[...] = jnp.exp2(change - shift)
        for k in range(rows // LANES):
            block = slice(k * LANES, (k + 1) * LANES)
            total = jnp.zeros((LANES, LANES), jnp.float32)
            for t in range(cols // LANES):
                total = total + plan_ref[block, t * LANES : (t + 1) * LANES] * factor[t : t + 1, :]
            totals[first + k : first + k + 1, :] = jnp.sum(total.T, axis=0, keepdims=True)
        part = slice(first, first + rows // LANES)
        total = totals[part, :]
        low = total if low is None else jnp.minimum(low, total)
        totals[part, :] = shift - row_ref[...] + jnp.log2(total)
    send(out_ref, totals[...])

    @pl.when(jnp.logical_not(smallest(low)[0, 0] >= SAFE))
    def _():
        wide = jnp.concatenate([potential[t : t + 1] for t in range(potential.shape[0])], axis=1)
        for index, (plan_ref, _, _, source_ref) in enumerate(blocks):
            count = plan_ref.shape[0] // LANES
            for k in range(count):
                part = score(source_ref[k * LANES : (k + 1) * LANES, :], half_ref[...], scale) + wide
                peak = jnp.max(part, axis=1, keepdims=True)
                total = jnp.sum(jnp.exp2(part - peak), axis=1, keepdims=True)
                row = index * count + k
                totals[row : row + 1, :] = jnp.broadcast_to(peak + jnp.log2(total), (LANES, LANES)).T[:1]
        send(out_ref, totals[...])


def scaled_columns(scale, potential, start_from, half_ref, blocks, out_ref, standing, folded):
    rows, cols = blocks[0][0].shape
    count = rows // LANES
    low = None
    results = list(start_from)
    for index, (plan_ref, row_ref, peak_ref, _) in enumerate(blocks):
        change = potential[index * count : (index + 1) * count] - row_ref[...]
        shift = largest(change)
        stand(standing, jnp.exp2(change - shift))
        total = column_sums(
            rows, cols, lambda block: plan_ref[block, :] * spread(standing[block, :], cols // LANES)
        )
        total = fold(folded, total)
        low = total if low is None else jnp.minimum(low, total)
        results.append(peak_ref[...] + shift + jnp.log2(total))
    send(out_ref, combine(jnp.stack(results)))

    @pl.when(jnp.logical_not(smallest(low)[0, 0] >= SAFE))
    def _():
        for start in range(0, cols, TILE):
            results = []
            for index, (_, _, _, source_ref) in enumerate(blocks):
                stand(standing, potential[index * count : (index + 1) * count])
                part = score(source_ref[...], half_ref[start : start + TILE, :], scale) + spread(
                    standing[...], TILE // LANES
                )
                peak = jnp.max(part, axis=0, keepdims=True)
                results.append(peak + jnp.log2(jnp.sum(jnp.exp2(part - peak), axis=0, keepdims=True)))
            result = combine(jnp.stack(results))
            for lane in range(0, TILE, LANES):
                t = (start + lane) // LANES
                folded[t : t + 1, :] = result[:, lane : lane + LANES]
        send(out_ref, combine(jnp.stack(list(start_from) + [folded[...]])))


def partner_columns(scale, columns_ref, potential_ref, half_ref, *refs):
    scaled_columns(scale, potential_ref[...], [columns_ref[...]], half_ref, (refs[:4],), *refs[4:])


def later_columns(scale, bits, gathered_ref, half_ref, *refs):
    potential = bits - combine(gathered_ref[...])
    scaled_columns(scale, potential, [], half_ref, (refs[:4], refs[4:8]), *refs[8:])


def finish(unit, row_bits, col_bits, row_parts_ref, column_parts_ref, row_ref, column_ref):
    row_ref[...] = unit * (col_bits - combine(row_parts_ref[...]))
    column_ref[...] = unit * (row_bits - combine(column_parts_ref[...]))


def local(source, target):
    f32 = jnp.float32
    own, width = source.shape
    first_plane = lax.axis_size(FIRST_PLANE)
    plane = lax.axis_size(PLANE)
    line = lax.axis_size(LINE)
    cores = lax.axis_size("core")
    rows = own * cores
    cols = target.shape[0] // cores
    row_bits = math.log2(rows * first_plane)
    col_bits = math.log2(cols * line)
    scale = math.log2(math.e) / (math.sqrt(width) * EPSILON)
    unit = EPSILON * math.log(2.0)
    core = lax.axis_index("core")
    swap = [(0, 1), (1, 0)]
    partner = [(0, 3), (3, 0), (1, 2), (2, 1)]
    vmem = pl.BlockSpec(memory_space=pltpu.VMEM)
    hbm = pl.BlockSpec(memory_space=pltpu.HBM)
    chip_shape = (rows // LANES, LANES)
    row_shape = (2 * rows // LANES, LANES)
    col_shape = (cols // LANES, LANES)
    limit = pltpu.CompilerParams(vmem_limit_bytes=24 * 2**20)
    block_out = [
        jax.ShapeDtypeStruct((rows, cols), f32),
        jax.ShapeDtypeStruct(chip_shape, f32),
        jax.ShapeDtypeStruct(col_shape, f32),
        jax.ShapeDtypeStruct((rows, width), source.dtype),
    ]

    half, rest = pl.pallas_call(
        fetch,
        in_specs=[hbm],
        out_specs=[vmem] * 2,
        out_shape=[jax.ShapeDtypeStruct((cols, width), target.dtype)] * 2,
        scratch_shapes=[pltpu.SemaphoreType.DMA((2,))],
        compiler_params=pltpu.CompilerParams(vmem_limit_bytes=51 * 2**20),
        name="fetch",
    )(target)
    parts, mine = pl.pallas_call(
        lambda *refs: first_rows(scale, *refs),
        in_specs=[vmem] * 3,
        out_specs=[vmem] * 2,
        out_shape=[
            jax.ShapeDtypeStruct((line, own // LANES, LANES), f32),
            jax.ShapeDtypeStruct((own, width), f32),
        ],
        scratch_shapes=[
            pltpu.VMEM((own, target.shape[0]), f32),
            pltpu.VMEM((own, LANES), f32),
            pltpu.VMEM((own // LANES, LANES), f32),
        ],
        compiler_params=limit,
        name="first_rows",
    )(source, half, rest)
    away = lax.ppermute(mine, ("p", "q"), partner)
    gathered = lax.all_to_all(parts, LINE, 0, 0)
    potential, mine, away = pl.pallas_call(
        lambda *refs: first_potential(col_bits, *refs),
        in_specs=[vmem] * 3,
        out_specs=[vmem] * 3,
        out_shape=[jax.ShapeDtypeStruct(chip_shape, f32)] + [jax.ShapeDtypeStruct((own, width), f32)] * 2,
        compiler_params=limit,
        name="first_potential",
    )(gathered, mine, away)
    other = lax.ppermute(mine, "core", swap)
    away_potential = lax.ppermute(potential, ("p", "q"), partner)
    columns, *mine_block = pl.pallas_call(
        lambda *refs: first_columns(scale, *refs),
        in_specs=[vmem] * 4,
        out_specs=[vmem] * 5,
        out_shape=[jax.ShapeDtypeStruct(col_shape, f32)] + block_out,
        scratch_shapes=[pltpu.VMEM((rows, LANES), f32), pltpu.VMEM(col_shape, f32)],
        compiler_params=limit,
        name="first_columns",
    )(mine, other, half, potential)
    away_block = pl.pallas_call(
        lambda *refs: partner_rows(scale, *refs),
        in_specs=[vmem] * 3,
        out_specs=[vmem] * 4,
        out_shape=block_out,
        compiler_params=limit,
        name="partner_rows",
    )(away, lax.ppermute(away, "core", swap), half)
    column_out = jax.ShapeDtypeStruct((plane,) + col_shape, f32)
    column_scratch = [pltpu.VMEM((rows, LANES), f32), pltpu.VMEM(col_shape, f32)]
    parts = pl.pallas_call(
        lambda *refs: partner_columns(scale, *refs),
        in_specs=[vmem] * 7,
        out_specs=vmem,
        out_shape=column_out,
        scratch_shapes=column_scratch,
        compiler_params=limit,
        name="partner_columns",
    )(columns, away_potential, half, *away_block)
    columns = lax.all_to_all(parts, PLANE, 0, 0)

    for step in range(1, ITERS):
        parts = pl.pallas_call(
            lambda *refs: later_rows(scale, row_bits, *refs),
            in_specs=[vmem] * 10,
            out_specs=vmem,
            out_shape=jax.ShapeDtypeStruct((line,) + row_shape, f32),
            scratch_shapes=[pltpu.VMEM(col_shape, f32), pltpu.VMEM(row_shape, f32)],
            compiler_params=limit,
            name="later_rows",
        )(columns, half, *mine_block, *away_block)
        gathered = lax.all_to_all(parts, LINE, 0, 0)
        parts = pl.pallas_call(
            lambda *refs: later_columns(scale, col_bits, *refs),
            in_specs=[vmem] * 10,
            out_specs=vmem,
            out_shape=column_out,
            scratch_shapes=column_scratch,
            compiler_params=limit,
            name="later_columns",
        )(gathered, half, *mine_block, *away_block)
        columns = lax.all_to_all(parts, PLANE, 0, 0)

    row_potential, column_potential = pl.pallas_call(
        lambda *refs: finish(unit, row_bits, col_bits, *refs),
        in_specs=[vmem] * 2,
        out_specs=[vmem] * 2,
        out_shape=[jax.ShapeDtypeStruct(row_shape, f32), jax.ShapeDtypeStruct(col_shape, f32)],
        compiler_params=limit,
        name="finish",
    )(gathered, columns)
    column_potential = column_potential.reshape(cols)
    other = lax.ppermute(column_potential, "core", swap)
    column_potential = jnp.where(
        core == 0,
        jnp.concatenate([column_potential, other]),
        jnp.concatenate([other, column_potential]),
    )
    row_potential = lax.dynamic_slice(row_potential.reshape(2 * rows), (core * own,), (own,))
    return (row_potential, column_potential)


def solution(mesh):
    fine = Mesh(mesh.devices.reshape(8, 2, 2, 2, 4), ("z", "p", "q", "core", "x"))
    return jax.shard_map(
        local,
        mesh=fine,
        in_specs=(P(("z", "p", "q", "core"), None), P("x", None)),
        out_specs=(P(("z", "p", "q", "core")), P("x")),
        check_vma=False,
    )
```

```python
import math

import jax
import jax.numpy as jnp
from jax import lax
from jax.experimental import pallas as pl
from jax.experimental.pallas import tpu as pltpu
from jax.sharding import Mesh, PartitionSpec as P

ITERS = 4
EPSILON = 0.1
TILE = 256
LANES = 128
SUBLANES = 8
CHUNKS = 4
SAFE = 2.0**-80

FIRST_PLANE = ("z", "p", "q")
PLANE = ("q", "z")
LINE = ("core", "x")


def combine(parts):
    peak = jnp.max(parts, axis=0)
    return peak + jnp.log2(jnp.sum(jnp.exp2(parts - peak[None]), axis=0))


def largest(values):
    return jnp.max(jnp.max(values, axis=1, keepdims=True), axis=0, keepdims=True)


def smallest(values):
    return jnp.min(jnp.min(values, axis=1, keepdims=True), axis=0, keepdims=True)


def stand(ref, values):
    for k in range(values.shape[0]):
        ref[k * LANES : (k + 1) * LANES, :] = jnp.broadcast_to(values[k : k + 1], (LANES, LANES)).T


def fold(ref, row):
    for k in range(ref.shape[0]):
        ref[k : k + 1, :] = row[:, k * LANES : (k + 1) * LANES]
    return ref[...]


def spread(row, count):
    return jnp.concatenate([row] * count, axis=1)


def send(out_ref, values):
    for slot in range(out_ref.shape[0]):
        out_ref[slot] = values


def score(source, target, scale):
    return scale * lax.dot_general(
        source, target, (((1,), (1,)), ((), ())), preferred_element_type=jnp.float32
    )


def first_rows(scale, source_ref, target_ref, out_ref, wide_ref, half_ref, rest_ref, scores, peaks, line, arrived):
    core = lax.axis_index("core")
    rows, half = source_ref.shape[0], half_ref.shape[0]
    chunk = half // CHUNKS
    copies = [
        pltpu.make_async_copy(
            target_ref.at[pl.ds(pl.multiple_of(side * half + k * chunk, chunk), chunk)],
            place.at[pl.ds(k * chunk, chunk)],
            arrived.at[index * CHUNKS + k],
        )
        for index, (side, place) in enumerate(((core, half_ref), (1 - core, rest_ref)))
        for k in range(CHUNKS)
    ]
    for copy in copies:
        copy.start()
    wide_ref[...] = source_ref[...].astype(jnp.float32)
    for start in range(0, 2 * half, TILE):
        if start % chunk == 0:
            copies[start // chunk].wait()
        place = half_ref if start < half else rest_ref
        tile = slice(start, start + TILE)
        part = score(source_ref[...], place[start % half : start % half + TILE, :], scale)
        scores[:, tile] = part
        high = part[:, :LANES]
        for lane in range(LANES, TILE, LANES):
            high = jnp.maximum(high, part[:, lane : lane + LANES])
        peaks[...] = high if start == 0 else jnp.maximum(peaks[...], high)
    for k in range(rows // LANES):
        block = slice(k * LANES, (k + 1) * LANES)
        peak = jnp.max(peaks[block, :], axis=1, keepdims=True)
        total = jnp.sum(jnp.exp2(scores[block, :] - peak), axis=1, keepdims=True)
        line[k : k + 1, :] = jnp.broadcast_to(peak + jnp.log2(total), (LANES, LANES)).T[:1]
    send(out_ref, line[...])


def column_sums(rows, width, get):
    total = lax.fori_loop(
        0,
        rows // SUBLANES,
        lambda k, total: total + get(pl.ds(pl.multiple_of(k * SUBLANES, SUBLANES), SUBLANES)),
        jnp.zeros((SUBLANES, width), jnp.float32),
        unroll=64,
    )
    return jnp.sum(total, axis=0, keepdims=True)


def place(source_ref, mine_ref, other_ref):
    core = lax.axis_index("core")
    own = mine_ref.shape[0]
    for side, piece in ((core, mine_ref), (1 - core, other_ref)):
        source_ref[pl.ds(pl.multiple_of(side * own, own), own), :] = piece[...].astype(source_ref.dtype)


def exponentials(scale, source_ref, half_ref, plan_ref, standing):
    rows, cols = plan_ref.shape
    highs = []
    for start in range(0, cols, TILE):
        tile = slice(start, start + TILE)
        part = score(source_ref[...], half_ref[tile, :], scale)
        if standing is not None:
            part = part + spread(standing[...], TILE // LANES)
        plan_ref[:, tile] = part
        highs.append(jnp.max(part, axis=0, keepdims=True))
    peak = jnp.concatenate(highs, axis=1)
    shift = jnp.broadcast_to(peak, (SUBLANES, cols))

    def term(block):
        value = jnp.exp2(plan_ref[block, :] - shift)
        plan_ref[block, :] = value
        return value

    return peak, column_sums(rows, cols, term)


def first_potential(bits, gathered_ref, mine_ref, away_ref, potential_ref, mine_out, away_out):
    mine_out[...] = mine_ref[...]
    away_out[...] = away_ref[...]
    parts = gathered_ref[...]
    each = parts.shape[0] // 2
    potential_ref[...] = bits - jnp.concatenate([combine(parts[:each]), combine(parts[each:])], axis=0)


def first_columns(
    scale,
    mine_ref,
    other_ref,
    half_ref,
    potential_ref,
    out_ref,
    plan_ref,
    row_ref,
    peak_ref,
    source_ref,
    standing,
    folded,
):
    place(source_ref, mine_ref, other_ref)
    row_ref[...] = potential_ref[...]
    stand(standing, potential_ref[...])
    peak, total = exponentials(scale, source_ref, half_ref, plan_ref, standing)
    out_ref[...] = fold(peak_ref, peak) + jnp.log2(fold(folded, total))


def partner_rows(
    scale, mine_ref, other_ref, half_ref, plan_ref, row_ref, peak_ref, source_ref
):
    place(source_ref, mine_ref, other_ref)
    row_ref[...] = jnp.zeros_like(row_ref)
    peak, _ = exponentials(scale, source_ref, half_ref, plan_ref, None)
    fold(peak_ref, peak)


def later_rows(scale, bits, gathered_ref, half_ref, *refs):
    blocks, (out_ref, factor, totals) = (refs[:4], refs[4:8]), refs[8:]
    potential = bits - combine(gathered_ref[...])
    low = None
    for index, (plan_ref, row_ref, peak_ref, _) in enumerate(blocks):
        rows, cols = plan_ref.shape
        first = index * rows // LANES
        change = potential + peak_ref[...]
        shift = largest(change)
        factor[...] = jnp.exp2(change - shift)
        for k in range(rows // LANES):
            block = slice(k * LANES, (k + 1) * LANES)
            total = jnp.zeros((LANES, LANES), jnp.float32)
            for t in range(cols // LANES):
                total = total + plan_ref[block, t * LANES : (t + 1) * LANES] * factor[t : t + 1, :]
            totals[first + k : first + k + 1, :] = jnp.sum(total.T, axis=0, keepdims=True)
        part = slice(first, first + rows // LANES)
        total = totals[part, :]
        low = total if low is None else jnp.minimum(low, total)
        totals[part, :] = shift - row_ref[...] + jnp.log2(total)
    send(out_ref, totals[...])

    @pl.when(jnp.logical_not(smallest(low)[0, 0] >= SAFE))
    def _():
        wide = jnp.concatenate([potential[t : t + 1] for t in range(potential.shape[0])], axis=1)
        for index, (plan_ref, _, _, source_ref) in enumerate(blocks):
            count = plan_ref.shape[0] // LANES
            for k in range(count):
                part = score(source_ref[k * LANES : (k + 1) * LANES, :], half_ref[...], scale) + wide
                peak = jnp.max(part, axis=1, keepdims=True)
                total = jnp.sum(jnp.exp2(part - peak), axis=1, keepdims=True)
                row = index * count + k
                totals[row : row + 1, :] = jnp.broadcast_to(peak + jnp.log2(total), (LANES, LANES)).T[:1]
        send(out_ref, totals[...])


def scaled_columns(scale, potential, start_from, half_ref, blocks, out_ref, standing, folded):
    rows, cols = blocks[0][0].shape
    count = rows // LANES
    low = None
    results = list(start_from)
    for index, (plan_ref, row_ref, peak_ref, _) in enumerate(blocks):
        change = potential[index * count : (index + 1) * count] - row_ref[...]
        shift = largest(change)
        stand(standing, jnp.exp2(change - shift))
        total = column_sums(
            rows, cols, lambda block: plan_ref[block, :] * spread(standing[block, :], cols // LANES)
        )
        total = fold(folded, total)
        low = total if low is None else jnp.minimum(low, total)
        results.append(peak_ref[...] + shift + jnp.log2(total))
    send(out_ref, combine(jnp.stack(results)))

    @pl.when(jnp.logical_not(smallest(low)[0, 0] >= SAFE))
    def _():
        for start in range(0, cols, TILE):
            results = []
            for index, (_, _, _, source_ref) in enumerate(blocks):
                stand(standing, potential[index * count : (index + 1) * count])
                part = score(source_ref[...], half_ref[start : start + TILE, :], scale) + spread(
                    standing[...], TILE // LANES
                )
                peak = jnp.max(part, axis=0, keepdims=True)
                results.append(peak + jnp.log2(jnp.sum(jnp.exp2(part - peak), axis=0, keepdims=True)))
            result = combine(jnp.stack(results))
            for lane in range(0, TILE, LANES):
                t = (start + lane) // LANES
                folded[t : t + 1, :] = result[:, lane : lane + LANES]
        send(out_ref, combine(jnp.stack(list(start_from) + [folded[...]])))


def partner_columns(scale, columns_ref, potential_ref, half_ref, *refs):
    scaled_columns(scale, potential_ref[...], [columns_ref[...]], half_ref, (refs[:4],), *refs[4:])


def later_columns(scale, bits, gathered_ref, half_ref, *refs):
    potential = bits - combine(gathered_ref[...])
    scaled_columns(scale, potential, [], half_ref, (refs[:4], refs[4:8]), *refs[8:])


def finish(unit, row_bits, col_bits, row_parts_ref, column_parts_ref, row_ref, column_ref):
    row_ref[...] = unit * (col_bits - combine(row_parts_ref[...]))
    column_ref[...] = unit * (row_bits - combine(column_parts_ref[...]))


def local(source, target):
    f32 = jnp.float32
    own, width = source.shape
    first_plane = lax.axis_size(FIRST_PLANE)
    plane = lax.axis_size(PLANE)
    line = lax.axis_size(LINE)
    cores = lax.axis_size("core")
    rows = own * cores
    cols = target.shape[0] // cores
    row_bits = math.log2(rows * first_plane)
    col_bits = math.log2(cols * line)
    scale = math.log2(math.e) / (math.sqrt(width) * EPSILON)
    unit = EPSILON * math.log(2.0)
    core = lax.axis_index("core")
    swap = [(0, 1), (1, 0)]
    partner = [(0, 3), (3, 0), (1, 2), (2, 1)]
    vmem = pl.BlockSpec(memory_space=pltpu.VMEM)
    hbm = pl.BlockSpec(memory_space=pltpu.HBM)
    chip_shape = (rows // LANES, LANES)
    row_shape = (2 * rows // LANES, LANES)
    col_shape = (cols // LANES, LANES)
    limit = pltpu.CompilerParams(vmem_limit_bytes=24 * 2**20)
    block_out = [
        jax.ShapeDtypeStruct((rows, cols), f32),
        jax.ShapeDtypeStruct(chip_shape, f32),
        jax.ShapeDtypeStruct(col_shape, f32),
        jax.ShapeDtypeStruct((rows, width), source.dtype),
    ]

    parts, mine, half = pl.pallas_call(
        lambda *refs: first_rows(scale, *refs),
        in_specs=[vmem, hbm],
        out_specs=[vmem] * 3,
        out_shape=[
            jax.ShapeDtypeStruct((line, own // LANES, LANES), f32),
            jax.ShapeDtypeStruct((own, width), f32),
            jax.ShapeDtypeStruct((cols, width), target.dtype),
        ],
        scratch_shapes=[
            pltpu.VMEM((cols, width), target.dtype),
            pltpu.VMEM((own, target.shape[0]), f32),
            pltpu.VMEM((own, LANES), f32),
            pltpu.VMEM((own // LANES, LANES), f32),
            pltpu.SemaphoreType.DMA((2 * CHUNKS,)),
        ],
        compiler_params=pltpu.CompilerParams(vmem_limit_bytes=52 * 2**20),
        name="first_rows",
    )(source, target)
    away = lax.ppermute(mine, ("p", "q"), partner)
    gathered = lax.all_to_all(parts, LINE, 0, 0)
    potential, mine, away = pl.pallas_call(
        lambda *refs: first_potential(col_bits, *refs),
        in_specs=[vmem] * 3,
        out_specs=[vmem] * 3,
        out_shape=[jax.ShapeDtypeStruct(chip_shape, f32)] + [jax.ShapeDtypeStruct((own, width), f32)] * 2,
        compiler_params=limit,
        name="first_potential",
    )(gathered, mine, away)
    other = lax.ppermute(mine, "core", swap)
    away_potential = lax.ppermute(potential, ("p", "q"), partner)
    columns, *mine_block = pl.pallas_call(
        lambda *refs: first_columns(scale, *refs),
        in_specs=[vmem] * 4,
        out_specs=[vmem] * 5,
        out_shape=[jax.ShapeDtypeStruct(col_shape, f32)] + block_out,
        scratch_shapes=[pltpu.VMEM((rows, LANES), f32), pltpu.VMEM(col_shape, f32)],
        compiler_params=limit,
        name="first_columns",
    )(mine, other, half, potential)
    away_block = pl.pallas_call(
        lambda *refs: partner_rows(scale, *refs),
        in_specs=[vmem] * 3,
        out_specs=[vmem] * 4,
        out_shape=block_out,
        compiler_params=limit,
        name="partner_rows",
    )(away, lax.ppermute(away, "core", swap), half)
    column_out = jax.ShapeDtypeStruct((plane,) + col_shape, f32)
    column_scratch = [pltpu.VMEM((rows, LANES), f32), pltpu.VMEM(col_shape, f32)]
    parts = pl.pallas_call(
        lambda *refs: partner_columns(scale, *refs),
        in_specs=[vmem] * 7,
        out_specs=vmem,
        out_shape=column_out,
        scratch_shapes=column_scratch,
        compiler_params=limit,
        name="partner_columns",
    )(columns, away_potential, half, *away_block)
    columns = lax.all_to_all(parts, PLANE, 0, 0)

    for step in range(1, ITERS):
        parts = pl.pallas_call(
            lambda *refs: later_rows(scale, row_bits, *refs),
            in_specs=[vmem] * 10,
            out_specs=vmem,
            out_shape=jax.ShapeDtypeStruct((line,) + row_shape, f32),
            scratch_shapes=[pltpu.VMEM(col_shape, f32), pltpu.VMEM(row_shape, f32)],
            compiler_params=limit,
            name="later_rows",
        )(columns, half, *mine_block, *away_block)
        gathered = lax.all_to_all(parts, LINE, 0, 0)
        parts = pl.pallas_call(
            lambda *refs: later_columns(scale, col_bits, *refs),
            in_specs=[vmem] * 10,
            out_specs=vmem,
            out_shape=column_out,
            scratch_shapes=column_scratch,
            compiler_params=limit,
            name="later_columns",
        )(gathered, half, *mine_block, *away_block)
        columns = lax.all_to_all(parts, PLANE, 0, 0)

    row_potential, column_potential = pl.pallas_call(
        lambda *refs: finish(unit, row_bits, col_bits, *refs),
        in_specs=[vmem] * 2,
        out_specs=[vmem] * 2,
        out_shape=[jax.ShapeDtypeStruct(row_shape, f32), jax.ShapeDtypeStruct(col_shape, f32)],
        compiler_params=limit,
        name="finish",
    )(gathered, columns)
    column_potential = column_potential.reshape(cols)
    other = lax.ppermute(column_potential, "core", swap)
    column_potential = jnp.where(
        core == 0,
        jnp.concatenate([column_potential, other]),
        jnp.concatenate([other, column_potential]),
    )
    row_potential = lax.dynamic_slice(row_potential.reshape(2 * rows), (core * own,), (own,))
    return (row_potential, column_potential)


def solution(mesh):
    fine = Mesh(mesh.devices.reshape(8, 2, 2, 2, 4), ("z", "p", "q", "core", "x"))
    return jax.shard_map(
        local,
        mesh=fine,
        in_specs=(P(("z", "p", "q", "core"), None), P("x", None)),
        out_specs=(P(("z", "p", "q", "core")), P("x")),
        check_vma=False,
    )
```

```python
import math

import jax
import jax.numpy as jnp
from jax import lax
from jax.experimental import pallas as pl
from jax.experimental.pallas import tpu as pltpu
from jax.sharding import Mesh, PartitionSpec as P

ITERS = 4
EPSILON = 0.1
TILE = 256
LANES = 128
SUBLANES = 8
SAFE = 2.0**-80

FIRST_PLANE = ("z", "p", "q")
PLANE = ("q", "z")
LINE = ("core", "x")


def combine(parts):
    peak = jnp.max(parts, axis=0)
    return peak + jnp.log2(jnp.sum(jnp.exp2(parts - peak[None]), axis=0))


def largest(values):
    return jnp.max(jnp.max(values, axis=1, keepdims=True), axis=0, keepdims=True)


def smallest(values):
    return jnp.min(jnp.min(values, axis=1, keepdims=True), axis=0, keepdims=True)


def stand(ref, values):
    for k in range(values.shape[0]):
        ref[k * LANES : (k + 1) * LANES, :] = jnp.broadcast_to(values[k : k + 1], (LANES, LANES)).T


def fold(ref, row):
    for k in range(ref.shape[0]):
        ref[k : k + 1, :] = row[:, k * LANES : (k + 1) * LANES]
    return ref[...]


def spread(row, count):
    return jnp.concatenate([row] * count, axis=1)


def send(out_ref, values):
    for slot in range(out_ref.shape[0]):
        out_ref[slot] = values


def score(source, target, scale):
    return scale * lax.dot_general(
        source, target, (((1,), (1,)), ((), ())), preferred_element_type=jnp.float32
    )


def fetch(target_ref, half_ref, rest_ref, arrived):
    core = lax.axis_index("core")
    half = half_ref.shape[0]
    copies = [
        pltpu.make_async_copy(target_ref.at[pl.ds(pl.multiple_of(side * half, half), half)], place, arrived.at[k])
        for k, (side, place) in enumerate(((core, half_ref), (1 - core, rest_ref)))
    ]
    for copy in copies:
        copy.start()
    for copy in copies:
        copy.wait()


def first_rows(scale, source_ref, half_ref, rest_ref, out_ref, wide_ref, scores, peaks, line):
    rows, half = source_ref.shape[0], half_ref.shape[0]
    wide_ref[...] = source_ref[...].astype(jnp.float32)
    for start in range(0, 2 * half, TILE):
        place = half_ref if start < half else rest_ref
        tile = slice(start, start + TILE)
        part = score(source_ref[...], place[start % half : start % half + TILE, :], scale)
        scores[:, tile] = part
        high = part[:, :LANES]
        for lane in range(LANES, TILE, LANES):
            high = jnp.maximum(high, part[:, lane : lane + LANES])
        peaks[...] = high if start == 0 else jnp.maximum(peaks[...], high)
    for k in range(rows // LANES):
        block = slice(k * LANES, (k + 1) * LANES)
        peak = jnp.max(peaks[block, :], axis=1, keepdims=True)
        total = jnp.sum(jnp.exp2(scores[block, :] - peak), axis=1, keepdims=True)
        line[k : k + 1, :] = jnp.broadcast_to(peak + jnp.log2(total), (LANES, LANES)).T[:1]
    send(out_ref, line[...])


def column_sums(rows, width, get):
    total = lax.fori_loop(
        0,
        rows // SUBLANES,
        lambda k, total: total + get(pl.ds(pl.multiple_of(k * SUBLANES, SUBLANES), SUBLANES)),
        jnp.zeros((SUBLANES, width), jnp.float32),
        unroll=64,
    )
    return jnp.sum(total, axis=0, keepdims=True)


def place(source_ref, mine_ref, other_ref):
    core = lax.axis_index("core")
    own = mine_ref.shape[0]
    for side, piece in ((core, mine_ref), (1 - core, other_ref)):
        source_ref[pl.ds(pl.multiple_of(side * own, own), own), :] = piece[...].astype(source_ref.dtype)


def exponentials(scale, source_ref, half_ref, plan_ref, standing):
    rows, cols = plan_ref.shape
    peaks, totals = [], []
    for start in range(0, cols, TILE):
        tile = slice(start, start + TILE)
        part = score(source_ref[...], half_ref[tile, :], scale)
        if standing is not None:
            part = part + spread(standing[...], TILE // LANES)
        plan_ref[:, tile] = part
        peak = jnp.max(part, axis=0, keepdims=True)
        shift = jnp.broadcast_to(peak, (SUBLANES, TILE))
        total = jnp.zeros((SUBLANES, TILE), jnp.float32)
        for row in range(0, rows, SUBLANES):
            block = slice(row, row + SUBLANES)
            value = jnp.exp2(plan_ref[block, tile] - shift)
            plan_ref[block, tile] = value
            total = total + value
        peaks.append(peak)
        totals.append(jnp.sum(total, axis=0, keepdims=True))
    return jnp.concatenate(peaks, axis=1), jnp.concatenate(totals, axis=1)


def first_potential(bits, gathered_ref, mine_ref, away_ref, potential_ref, mine_out, away_out):
    mine_out[...] = mine_ref[...]
    away_out[...] = away_ref[...]
    parts = gathered_ref[...]
    each = parts.shape[0] // 2
    potential_ref[...] = bits - jnp.concatenate([combine(parts[:each]), combine(parts[each:])], axis=0)


def first_columns(
    scale,
    mine_ref,
    other_ref,
    half_ref,
    potential_ref,
    out_ref,
    plan_ref,
    row_ref,
    peak_ref,
    source_ref,
    standing,
    folded,
):
    place(source_ref, mine_ref, other_ref)
    row_ref[...] = potential_ref[...]
    stand(standing, potential_ref[...])
    peak, total = exponentials(scale, source_ref, half_ref, plan_ref, standing)
    out_ref[...] = fold(peak_ref, peak) + jnp.log2(fold(folded, total))


def partner_rows(
    scale, mine_ref, other_ref, half_ref, plan_ref, row_ref, peak_ref, source_ref
):
    place(source_ref, mine_ref, other_ref)
    row_ref[...] = jnp.zeros_like(row_ref)
    peak, _ = exponentials(scale, source_ref, half_ref, plan_ref, None)
    fold(peak_ref, peak)


def later_rows(scale, bits, gathered_ref, half_ref, *refs):
    blocks, (out_ref, factor, totals) = (refs[:4], refs[4:8]), refs[8:]
    potential = bits - combine(gathered_ref[...])
    low = None
    for index, (plan_ref, row_ref, peak_ref, _) in enumerate(blocks):
        rows, cols = plan_ref.shape
        first = index * rows // LANES
        change = potential + peak_ref[...]
        shift = largest(change)
        factor[...] = jnp.exp2(change - shift)
        for k in range(rows // LANES):
            block = slice(k * LANES, (k + 1) * LANES)
            total = jnp.zeros((LANES, LANES), jnp.float32)
            for t in range(cols // LANES):
                total = total + plan_ref[block, t * LANES : (t + 1) * LANES] * factor[t : t + 1, :]
            totals[first + k : first + k + 1, :] = jnp.sum(total.T, axis=0, keepdims=True)
        part = slice(first, first + rows // LANES)
        total = totals[part, :]
        low = total if low is None else jnp.minimum(low, total)
        totals[part, :] = shift - row_ref[...] + jnp.log2(total)
    send(out_ref, totals[...])

    @pl.when(jnp.logical_not(smallest(low)[0, 0] >= SAFE))
    def _():
        wide = jnp.concatenate([potential[t : t + 1] for t in range(potential.shape[0])], axis=1)
        for index, (plan_ref, _, _, source_ref) in enumerate(blocks):
            count = plan_ref.shape[0] // LANES
            for k in range(count):
                part = score(source_ref[k * LANES : (k + 1) * LANES, :], half_ref[...], scale) + wide
                peak = jnp.max(part, axis=1, keepdims=True)
                total = jnp.sum(jnp.exp2(part - peak), axis=1, keepdims=True)
                row = index * count + k
                totals[row : row + 1, :] = jnp.broadcast_to(peak + jnp.log2(total), (LANES, LANES)).T[:1]
        send(out_ref, totals[...])


def scaled_columns(scale, potential, start_from, half_ref, blocks, out_ref, standing, folded):
    rows, cols = blocks[0][0].shape
    count = rows // LANES
    low = None
    results = list(start_from)
    for index, (plan_ref, row_ref, peak_ref, _) in enumerate(blocks):
        change = potential[index * count : (index + 1) * count] - row_ref[...]
        shift = largest(change)
        stand(standing, jnp.exp2(change - shift))
        total = column_sums(
            rows, cols, lambda block: plan_ref[block, :] * spread(standing[block, :], cols // LANES)
        )
        total = fold(folded, total)
        low = total if low is None else jnp.minimum(low, total)
        results.append(peak_ref[...] + shift + jnp.log2(total))
    send(out_ref, combine(jnp.stack(results)))

    @pl.when(jnp.logical_not(smallest(low)[0, 0] >= SAFE))
    def _():
        for start in range(0, cols, TILE):
            results = []
            for index, (_, _, _, source_ref) in enumerate(blocks):
                stand(standing, potential[index * count : (index + 1) * count])
                part = score(source_ref[...], half_ref[start : start + TILE, :], scale) + spread(
                    standing[...], TILE // LANES
                )
                peak = jnp.max(part, axis=0, keepdims=True)
                results.append(peak + jnp.log2(jnp.sum(jnp.exp2(part - peak), axis=0, keepdims=True)))
            result = combine(jnp.stack(results))
            for lane in range(0, TILE, LANES):
                t = (start + lane) // LANES
                folded[t : t + 1, :] = result[:, lane : lane + LANES]
        send(out_ref, combine(jnp.stack(list(start_from) + [folded[...]])))


def partner_columns(scale, columns_ref, potential_ref, half_ref, *refs):
    scaled_columns(scale, potential_ref[...], [columns_ref[...]], half_ref, (refs[:4],), *refs[4:])


def later_columns(scale, bits, gathered_ref, half_ref, *refs):
    potential = bits - combine(gathered_ref[...])
    scaled_columns(scale, potential, [], half_ref, (refs[:4], refs[4:8]), *refs[8:])


def finish(unit, row_bits, col_bits, row_parts_ref, column_parts_ref, row_ref, column_ref):
    row_ref[...] = unit * (col_bits - combine(row_parts_ref[...]))
    column_ref[...] = unit * (row_bits - combine(column_parts_ref[...]))


def local(source, target):
    f32 = jnp.float32
    own, width = source.shape
    first_plane = lax.axis_size(FIRST_PLANE)
    plane = lax.axis_size(PLANE)
    line = lax.axis_size(LINE)
    cores = lax.axis_size("core")
    rows = own * cores
    cols = target.shape[0] // cores
    row_bits = math.log2(rows * first_plane)
    col_bits = math.log2(cols * line)
    scale = math.log2(math.e) / (math.sqrt(width) * EPSILON)
    unit = EPSILON * math.log(2.0)
    core = lax.axis_index("core")
    swap = [(0, 1), (1, 0)]
    partner = [(0, 3), (3, 0), (1, 2), (2, 1)]
    vmem = pl.BlockSpec(memory_space=pltpu.VMEM)
    hbm = pl.BlockSpec(memory_space=pltpu.HBM)
    chip_shape = (rows // LANES, LANES)
    row_shape = (2 * rows // LANES, LANES)
    col_shape = (cols // LANES, LANES)
    limit = pltpu.CompilerParams(vmem_limit_bytes=24 * 2**20)
    block_out = [
        jax.ShapeDtypeStruct((rows, cols), f32),
        jax.ShapeDtypeStruct(chip_shape, f32),
        jax.ShapeDtypeStruct(col_shape, f32),
        jax.ShapeDtypeStruct((rows, width), source.dtype),
    ]

    half, rest = pl.pallas_call(
        fetch,
        in_specs=[hbm],
        out_specs=[vmem] * 2,
        out_shape=[jax.ShapeDtypeStruct((cols, width), target.dtype)] * 2,
        scratch_shapes=[pltpu.SemaphoreType.DMA((2,))],
        compiler_params=pltpu.CompilerParams(vmem_limit_bytes=51 * 2**20),
        name="fetch",
    )(target)
    parts, mine = pl.pallas_call(
        lambda *refs: first_rows(scale, *refs),
        in_specs=[vmem] * 3,
        out_specs=[vmem] * 2,
        out_shape=[
            jax.ShapeDtypeStruct((line, own // LANES, LANES), f32),
            jax.ShapeDtypeStruct((own, width), f32),
        ],
        scratch_shapes=[
            pltpu.VMEM((own, target.shape[0]), f32),
            pltpu.VMEM((own, LANES), f32),
            pltpu.VMEM((own // LANES, LANES), f32),
        ],
        compiler_params=limit,
        name="first_rows",
    )(source, half, rest)
    away = lax.ppermute(mine, ("p", "q"), partner)
    gathered = lax.all_to_all(parts, LINE, 0, 0)
    potential, mine, away = pl.pallas_call(
        lambda *refs: first_potential(col_bits, *refs),
        in_specs=[vmem] * 3,
        out_specs=[vmem] * 3,
        out_shape=[jax.ShapeDtypeStruct(chip_shape, f32)] + [jax.ShapeDtypeStruct((own, width), f32)] * 2,
        compiler_params=limit,
        name="first_potential",
    )(gathered, mine, away)
    other = lax.ppermute(mine, "core", swap)
    away_potential = lax.ppermute(potential, ("p", "q"), partner)
    columns, *mine_block = pl.pallas_call(
        lambda *refs: first_columns(scale, *refs),
        in_specs=[vmem] * 4,
        out_specs=[vmem] * 5,
        out_shape=[jax.ShapeDtypeStruct(col_shape, f32)] + block_out,
        scratch_shapes=[pltpu.VMEM((rows, LANES), f32), pltpu.VMEM(col_shape, f32)],
        compiler_params=limit,
        name="first_columns",
    )(mine, other, half, potential)
    away_block = pl.pallas_call(
        lambda *refs: partner_rows(scale, *refs),
        in_specs=[vmem] * 3,
        out_specs=[vmem] * 4,
        out_shape=block_out,
        compiler_params=limit,
        name="partner_rows",
    )(away, lax.ppermute(away, "core", swap), half)
    column_out = jax.ShapeDtypeStruct((plane,) + col_shape, f32)
    column_scratch = [pltpu.VMEM((rows, LANES), f32), pltpu.VMEM(col_shape, f32)]
    parts = pl.pallas_call(
        lambda *refs: partner_columns(scale, *refs),
        in_specs=[vmem] * 7,
        out_specs=vmem,
        out_shape=column_out,
        scratch_shapes=column_scratch,
        compiler_params=limit,
        name="partner_columns",
    )(columns, away_potential, half, *away_block)
    columns = lax.all_to_all(parts, PLANE, 0, 0)

    for step in range(1, ITERS):
        parts = pl.pallas_call(
            lambda *refs: later_rows(scale, row_bits, *refs),
            in_specs=[vmem] * 10,
            out_specs=vmem,
            out_shape=jax.ShapeDtypeStruct((line,) + row_shape, f32),
            scratch_shapes=[pltpu.VMEM(col_shape, f32), pltpu.VMEM(row_shape, f32)],
            compiler_params=limit,
            name="later_rows",
        )(columns, half, *mine_block, *away_block)
        gathered = lax.all_to_all(parts, LINE, 0, 0)
        parts = pl.pallas_call(
            lambda *refs: later_columns(scale, col_bits, *refs),
            in_specs=[vmem] * 10,
            out_specs=vmem,
            out_shape=column_out,
            scratch_shapes=column_scratch,
            compiler_params=limit,
            name="later_columns",
        )(gathered, half, *mine_block, *away_block)
        columns = lax.all_to_all(parts, PLANE, 0, 0)

    row_potential, column_potential = pl.pallas_call(
        lambda *refs: finish(unit, row_bits, col_bits, *refs),
        in_specs=[vmem] * 2,
        out_specs=[vmem] * 2,
        out_shape=[jax.ShapeDtypeStruct(row_shape, f32), jax.ShapeDtypeStruct(col_shape, f32)],
        compiler_params=limit,
        name="finish",
    )(gathered, columns)
    column_potential = column_potential.reshape(cols)
    other = lax.ppermute(column_potential, "core", swap)
    column_potential = jnp.where(
        core == 0,
        jnp.concatenate([column_potential, other]),
        jnp.concatenate([other, column_potential]),
    )
    row_potential = lax.dynamic_slice(row_potential.reshape(2 * rows), (core * own,), (own,))
    return (row_potential, column_potential)


def solution(mesh):
    fine = Mesh(mesh.devices.reshape(8, 2, 2, 2, 4), ("z", "p", "q", "core", "x"))
    return jax.shard_map(
        local,
        mesh=fine,
        in_specs=(P(("z", "p", "q", "core"), None), P("x", None)),
        out_specs=(P(("z", "p", "q", "core")), P("x")),
        check_vma=False,
    )
```
